32 devices in a mesh: layer: 4 (over z), feat: 8 (over y, x, core).
Axes of the slice: x: 2, y: 2, z: 4, core: 2. Of those that a mesh axis runs over, the one named last changes fastest.
Arguments:
- resid: bfloat16 [8, 256, 4096], P('layer', None, 'feat'), may hold values from -6 to 6
- enc: bfloat16 [8, 4096, 4096], P('layer', None, 'feat'), may hold values from -0.09375 to 0.09375
- enc_bias: float32 [8, 4096], P('layer', 'feat'), may hold values from -3 to 3
- fire: int32 [8, 256, 4096], P('layer', None, 'feat'), may hold values 0 or 1
- dec: bfloat16 [36, 4096, 4096], P('layer', 'feat'), may hold values from -0.125 to 0.125
- dec_bias: bfloat16 [8, 4096], P('layer', 'feat'), may hold values from -2 to 2
- target: bfloat16 [8, 256, 4096], P('layer', None, 'feat'), may hold values from -6 to 6
Outputs:
- error: bfloat16 [8, 256, 4096], P('layer', None, 'feat')
- act_grad: float32 [8, 256, 4096], P('layer', None, 'feat')
The draws below stay inside these ranges and needn't reach their ends.
All inputs are finite; a program needn't handle non-finite values. No bound on the sum of `fire` on one device may be relied on, other than what follows from the above.
Results may differ from the reference program's by a relative error of at most 0.0085.
Values may be sent and summed in bfloat16 or wider, within the bound.
No kernel may reach another device: no remote copies, remote signals or barrier semaphores. Data moves between devices by JAX's collectives and lax.ppermute only.
A program may use at most 192 MiB of HBM per device.

```python
import jax
import jax.numpy as jnp
from jax import lax

D = 4096
F = 4096
LAYERS = 8
TOK = 256
PAIRS = 36


def touch_ends(values, rng, least, high):
    place = [jax.random.randint(jax.random.fold_in(rng, axis), (), 0, length) for axis, length in enumerate(values.shape)]
    widest = values.shape.index(max(values.shape))
    beside = place[:widest] + [(place[widest] + 1) % values.shape[widest]] + place[widest + 1:]
    return values.at[tuple(place)].set(least).at[tuple(beside)].set(high)


def raised(array, rng, source, target, shards_of, factor):
    def block_of(position):
        return (jnp.arange(array.shape[position]) // (array.shape[position] // shards_of)).reshape((-1,) + (1,) * (array.ndim - 1 - position))

    first = jax.random.permutation(rng, shards_of)[block_of(target)]
    other_side = (block_of(target) + shards_of // 2) % shards_of
    return jnp.where((block_of(source) == first) | (block_of(source) == other_side), factor * array, array)


def level_of(key, extent, pieces, low, top_value):
    def one(position, shards_of):
        draws = jax.random.uniform(jax.random.fold_in(jax.random.fold_in(key, 6), position), (shards_of,), jnp.float32, low / len(pieces), top_value / len(pieces))
        return jnp.repeat(jnp.exp(draws), extent[position] // shards_of).reshape((-1,) + (1,) * (len(extent) - position - 1))

    loudness = one(*pieces[0])
    for cut in pieces[1:]:
        loudness = loudness * one(*cut)
    return loudness


def centred(rng, dims, scale, limit, shards=(), kind=jnp.bfloat16):
    drawn = jax.random.normal(rng, dims, jnp.float32) * scale
    if len(shards) > 0:
        drawn = level_of(rng, dims, shards, -0.22, 0.18) * drawn
    return jnp.clip(drawn, min=-limit, max=limit).astype(kind)


def heavy_noise(own_key, extent, width, bound, split, heavy, held_as=jnp.bfloat16):
    drawn = width * jax.random.normal(own_key, extent, jnp.float32)
    if split:
        drawn = drawn * level_of(own_key, extent, split, -0.22, 0.18)
    return jnp.clip(raised(drawn, jax.random.fold_in(own_key, 3), *heavy), -bound, bound).astype(held_as)


def setup_inputs(seed: int = 0) -> dict:
    key_list = jax.random.split(jax.random.key(seed), 8)
    resid = centred(key_list[0], (LAYERS, TOK, D), 1.0, 6.0, ((0, 4), (2, 8)))
    enc = centred(key_list[1], (LAYERS, D, F), D ** -0.5, 0.09375, ((0, 4), (2, 8)))
    enc_bias = centred(key_list[2], (LAYERS, F), 0.5, 3.0, ((0, 4), (1, 8)), jnp.float32)
    fire = touch_ends((jax.random.randint(key_list[3], (LAYERS, TOK, F), 0, 4) < 1).astype(jnp.int32), jax.random.fold_in(key_list[3], 1), 0, 1)
    dec = heavy_noise(key_list[4], (PAIRS, F, D), F ** -0.5, 0.125, ((0, 4), (1, 8)), (1, 2, 8, 2.0))
    dec_bias = centred(key_list[5], (LAYERS, D), 0.3, 2.0, ((0, 4), (1, 8)))
    target = centred(key_list[6], (LAYERS, TOK, D), 1.0, 6.0, ((0, 4), (2, 8)))
    return {"resid": resid, "enc": enc, "enc_bias": enc_bias, "fire": fire, "dec": dec, "dec_bias": dec_bias, "target": target}


def pair_table():
    rows = []
    for group in range(LAYERS // 2):
        for k in range(LAYERS + 1):
            if k <= group:
                rows.append((k, 2 * group))
            else:
                rows.append((k - group - 1, 2 * group + 1))
    return rows


def reference(resid, enc, enc_bias, fire, dec, dec_bias, target):
    acts = []
    for layer in range(LAYERS):
        pre = jnp.dot(resid[layer], enc[layer], preferred_element_type=jnp.float32) + enc_bias[layer]
        acts.append((fire[layer].astype(jnp.float32) * pre).astype(jnp.bfloat16))
    table = pair_table()
    recon = [jnp.zeros((TOK, D), jnp.float32) for _ in range(LAYERS)]
    for pair, (source, slot) in enumerate(table):
        recon[slot] = recon[slot] + jnp.dot(acts[source], dec[pair], preferred_element_type=jnp.float32)
    errors = []
    for slot in range(LAYERS):
        value = recon[slot] + dec_bias[slot].astype(jnp.float32) - target[slot].astype(jnp.float32)
        errors.append(value.astype(jnp.bfloat16))
    grads = [jnp.zeros((TOK, F), jnp.float32) for _ in range(LAYERS)]
    for pair, (source, slot) in enumerate(table):
        term = lax.dot_general(errors[slot], dec[pair], (((1,), (1,)), ((), ())), preferred_element_type=jnp.float32)
        grads[source] = grads[source] + term
    act_grad = jnp.stack([fire[layer].astype(jnp.float32) * grads[layer] for layer in range(LAYERS)])
    return jnp.stack(errors), act_grad
```

```python
import jax
import jax.numpy as jnp
from jax import lax
from jax.experimental import pallas as pl
from jax.experimental.pallas import tpu as pltpu
from jax.sharding import PartitionSpec as P

LAYERS = 8
CHUNKS = 1
VMEM = pl.BlockSpec(memory_space=pltpu.VMEM)
SMEM = pl.BlockSpec(memory_space=pltpu.SMEM)
LIMIT = 48 * 2**20


def plain(resid, enc, enc_bias, fire, dec, dec_bias, target):
    group = lax.axis_index("layer")
    half = LAYERS // 2
    pre = jnp.einsum(
        "ltd,ldf->ltf",
        lax.all_gather(resid, "feat", axis=2, tiled=True),
        enc,
        preferred_element_type=jnp.float32,
    )
    acts = (fire.astype(jnp.float32) * (pre + enc_bias[:, None, :])).astype(jnp.bfloat16)
    every = lax.all_gather(acts, "layer", axis=0, tiled=True)
    order = jnp.arange(LAYERS + 1, dtype=jnp.int32)
    early = order <= group
    source_ids = jnp.where(early, order, order - group - 1)
    chosen = jnp.take(every, source_ids, axis=0)
    lead_mask = early[:half].astype(jnp.bfloat16)[:, None, None]
    lead_acts = chosen[:half]
    low = jnp.einsum(
        "ktf,kfd->td", lead_acts * lead_mask, dec[:half], preferred_element_type=jnp.float32
    )
    high = jnp.einsum(
        "ktf,kfd->td", lead_acts * (1 - lead_mask), dec[:half], preferred_element_type=jnp.float32
    )
    high = high + jnp.einsum(
        "ktf,kfd->td", chosen[half:], dec[half:], preferred_element_type=jnp.float32
    )
    partial_value = jnp.stack([low, high])
    recon = lax.psum(partial_value, "feat")
    whole_target, whole_bias = (
        lax.all_gather(target, "feat", axis=2, tiled=True),
        lax.all_gather(dec_bias, "feat", axis=1, tiled=True),
    )
    wide_error = (
        recon + whole_bias.astype(jnp.float32)[:, None, :] - whole_target.astype(jnp.float32)
    ).astype(jnp.bfloat16)
    columns = target.shape[2]
    error = lax.dynamic_slice_in_dim(wide_error, lax.axis_index("feat") * columns, columns, 2)
    lead_error = jnp.where(early[:half, None, None], wide_error[0][None], wide_error[1][None])
    grads_lead = jnp.einsum(
        "ktd,kfd->ktf", lead_error, dec[:half], preferred_element_type=jnp.float32
    )
    grads_rest = jnp.einsum(
        "td,kfd->ktf", wide_error[1], dec[half:], preferred_element_type=jnp.float32
    )
    pair_grads = jnp.concatenate([grads_lead, grads_rest], axis=0)
    one_hot = (source_ids[:, None] == jnp.arange(LAYERS, dtype=jnp.int32)[None, :]).astype(
        jnp.float32
    )
    grad_terms = jnp.einsum("ks,ktf->stf", one_hot, pair_grads, precision=lax.Precision.HIGHEST)
    summed = lax.psum_scatter(
        grad_terms.astype(jnp.bfloat16), "layer", scatter_dimension=0, tiled=True
    ).astype(jnp.float32)
    act_grad = fire.astype(jnp.float32) * summed
    return (error, act_grad)


def pre_kernel(order, *refs):
    *blocks, enc, bias, fire, out, acc = refs
    width = blocks[0].shape[2]
    layer = pl.program_id(0)
    for i, block in enumerate(blocks):
        rows = pl.ds(pl.multiple_of(order[i] * width, width), width)
        term = jnp.dot(block[layer], enc[0, rows, :], preferred_element_type=jnp.float32)
        if i == 0:
            acc[...] = term
        else:
            acc[...] += term
    out[0] = (fire[0].astype(jnp.float32) * (acc[...] + bias[0])).astype(jnp.bfloat16)


def encode(order, blocks, enc, bias, fire, chunk):
    layers, tokens, _ = blocks[0].shape
    _, depth, feats = enc.shape
    part = feats // 2
    return pl.pallas_call(
        pre_kernel,
        grid=(layers, feats // part),
        in_specs=[SMEM]
        + [VMEM] * len(blocks)
        + [
            pl.BlockSpec((1, depth, part), lambda l, h: (l, 0, h)),
            pl.BlockSpec((1, 1, part), lambda l, h: (l, 0, h)),
            pl.BlockSpec((1, tokens, part), lambda l, h: (l, chunk, h)),
        ],
        out_specs=pl.BlockSpec((1, tokens, part), lambda l, h: (l, 0, h)),
        out_shape=jax.ShapeDtypeStruct((layers, tokens, feats), jnp.bfloat16),
        scratch_shapes=[pltpu.VMEM((tokens, part), jnp.float32)],
        compiler_params=pltpu.CompilerParams(vmem_limit_bytes=LIMIT),
        cost_estimate=pl.CostEstimate(
            flops=2 * layers * tokens * depth * feats, bytes_accessed=2 * enc.size, transcendentals=0
        ),
        name="encode",
    )(order, *blocks, enc, bias, fire)


def rec_kernel(cols, rows, edge, *refs):
    *sources, dec, keep, send, held, acc = refs
    k = pl.program_id(0)
    width = keep.shape[3]
    layers = keep.shape[1]
    quarter = dec.shape[2] // 4

    @pl.when(k == 0)
    def _():
        for i, source in enumerate(sources):
            held[layers * i : layers * (i + 1)] = source[...]
        acc[...] = jnp.zeros_like(acc)

    slot = (k >= edge[0]).astype(jnp.int32)
    acts = held[rows[k]]
    for j in range(4):
        part = slice(j * quarter, (j + 1) * quarter)
        acc[slot, :, part] += jnp.dot(acts, dec[0, :, part], preferred_element_type=jnp.float32)

    @pl.when(k == pl.num_programs(0) - 1)
    def _():
        for i in range(8):
            place = pl.ds(pl.multiple_of(cols[i] * width, width), width)
            for s in range(layers):
                value = acc[s, :, place].astype(jnp.bfloat16)
                if i < 4:
                    keep[i, s] = value
                else:
                    send[i - 4, s] = value


def reconstruct(cols, rows, edge, sources, dec):
    layers, tokens, feats = sources[0].shape
    pairs, _, depth = dec.shape
    out = jax.ShapeDtypeStruct((4, layers, tokens, depth // 8), jnp.bfloat16)
    return pl.pallas_call(
        rec_kernel,
        grid=(pairs,),
        in_specs=[SMEM] * 3
        + [VMEM] * len(sources)
        + [pl.BlockSpec((1, feats, depth), lambda k: (k, 0, 0))],
        out_specs=[VMEM, VMEM],
        out_shape=[out, out],
        scratch_shapes=[
            pltpu.VMEM((layers * len(sources), tokens, feats), jnp.bfloat16),
            pltpu.VMEM((layers, tokens, depth), jnp.float32),
        ],
        compiler_params=pltpu.CompilerParams(vmem_limit_bytes=LIMIT),
        cost_estimate=pl.CostEstimate(
            flops=2 * tokens * dec.size, bytes_accessed=2 * dec.size, transcendentals=0
        ),
        name="reconstruct",
    )(cols, rows, edge, *sources, dec)


def grad_kernel(cols, rows, edge, *refs):
    blocks, dec, outs, error, total = refs[:8], refs[8], refs[9:-2], refs[-2], refs[-1]
    k = pl.program_id(0)
    width = blocks[0].shape[2]
    layers = blocks[0].shape[0]

    @pl.when(k == 0)
    def _():
        for i, block in enumerate(blocks):
            place = pl.ds(pl.multiple_of(cols[i] * width, width), width)
            error[:, :, place] = block[...]
        total[...] = jnp.zeros_like(total)

    slot = (k >= edge[0]).astype(jnp.int32)
    total[rows[k]] += lax.dot_general(
        error[slot], dec[0], (((1,), (1,)), ((), ())), preferred_element_type=jnp.float32
    )

    @pl.when(k == pl.num_programs(0) - 1)
    def _():
        for i, out in enumerate(outs):
            out[...] = total[layers * i : layers * (i + 1)].astype(out.dtype)


def gradients(cols, rows, edge, blocks, dec):
    layers, tokens, _ = blocks[0].shape
    pairs, feats, depth = dec.shape
    return pl.pallas_call(
        grad_kernel,
        grid=(pairs,),
        in_specs=[SMEM] * 3
        + [VMEM] * len(blocks)
        + [pl.BlockSpec((1, feats, depth), lambda k: (k, 0, 0))],
        out_specs=[VMEM] * 7,
        out_shape=[
            jax.ShapeDtypeStruct((layers, tokens, feats), jnp.bfloat16 if i else jnp.float32)
            for i in range(7)
        ],
        scratch_shapes=[
            pltpu.VMEM((layers, tokens, depth), jnp.bfloat16),
            pltpu.VMEM((layers * 7, tokens, feats), jnp.float32),
        ],
        compiler_params=pltpu.CompilerParams(vmem_limit_bytes=LIMIT),
        cost_estimate=pl.CostEstimate(
            flops=2 * tokens * dec.size, bytes_accessed=2 * dec.size, transcendentals=0
        ),
        name="gradients",
    )(cols, rows, edge, *blocks, dec)


FLIP = [(i, i ^ 1) for i in range(8)]
FIRST = [(i, i ^ (4 if i & 1 else 2)) for i in range(8)]
SECOND = [(i, i ^ (2 if i & 1 else 4)) for i in range(8)]
UP = [(i, i + 1) for i in range(3)]
DOWN = [(i + 1, i) for i in range(3)]


def gather(own):
    first = lax.ppermute(own, "feat", FIRST)
    second = lax.ppermute(own, "feat", SECOND)
    both = lax.ppermute(first, "feat", SECOND)
    mine = [own, first, second, both]
    return mine + [lax.ppermute(b, "feat", FLIP) for b in mine]


def on_device(resid, enc, enc_bias, fire, dec, dec_bias, target):
    group = lax.axis_index("layer")
    me = lax.axis_index("feat")
    core = me & 1
    one, two = 2 + 2 * core, 4 - 2 * core
    gathered = jnp.stack([0 * core, one, two, 0 * core + 6, 0 * core + 1, two ^ 1, one ^ 1, 0 * core + 7])
    columns = (me ^ gathered).astype(jnp.int32)
    scattered = columns
    k = jnp.arange(LAYERS + 1, dtype=jnp.int32)
    source = jnp.where(k <= group, k, k - group - 1)
    away = source // 2 - group
    place = jnp.where(away >= 0, away, 3 - away)
    rows = (2 * place + source % 2).astype(jnp.int32)
    edge = (group + 1).astype(jnp.int32)[None]
    bias3 = enc_bias[:, None, :]
    tokens = resid.shape[1] // CHUNKS
    errors, grads = [], []
    for c in range(CHUNKS):
        span = slice(c * tokens, (c + 1) * tokens)
        blocks = gather(resid[:, span])
        acts = encode(columns, blocks, enc, bias3, fire, c)
        above1 = lax.ppermute(acts, "layer", DOWN)
        below1 = lax.ppermute(acts, "layer", UP)
        above2 = lax.ppermute(above1, "layer", [(1, 0), (2, 1)])
        below2 = lax.ppermute(below1, "layer", [(1, 2), (2, 3)])
        above3 = lax.ppermute(acts, "layer", [(3, 0)])
        below3 = lax.ppermute(acts, "layer", [(0, 3)])
        keep, send = reconstruct(
            scattered, rows, edge, [acts, above1, above2, above3, below1, below2, below3], dec
        )
        other = lax.ppermute(send, "feat", FLIP)
        f32 = jnp.float32
        pair = keep.astype(f32) + other.astype(f32)
        far = lax.ppermute(pair[2:].astype(jnp.bfloat16), "feat", SECOND).astype(f32)
        near = lax.ppermute((pair[1] + far[1]).astype(jnp.bfloat16), "feat", FIRST).astype(f32)
        recon = pair[0] + far[0] + near
        error = (
            recon + dec_bias.astype(f32)[:, None, :] - target[:, span].astype(f32)
        ).astype(jnp.bfloat16)
        errors.append(error)
        own, up1, up2, up3, down1, down2, down3 = gradients(columns, rows, edge, gather(error), dec)
        up3 = lax.ppermute(up3, "layer", [(0, 3)])
        down3 = lax.ppermute(down3, "layer", [(3, 0)])
        up2 = lax.ppermute(up2, "layer", [(0, 1), (1, 2)]).astype(f32)
        down2 = lax.ppermute(down2, "layer", [(3, 2), (2, 1)]).astype(f32)
        up1 = lax.ppermute((up1.astype(f32) + up2).astype(jnp.bfloat16), "layer", UP)
        down1 = lax.ppermute((down1.astype(f32) + down2).astype(jnp.bfloat16), "layer", DOWN)
        total = own + up1.astype(f32) + down1.astype(f32) + up3.astype(f32) + down3.astype(f32)
        grads.append(fire[:, span].astype(f32) * total)
    return jnp.concatenate(errors, axis=1), jnp.concatenate(grads, axis=1)


def solution(mesh):
    placed = (
        P("layer", None, "feat"),
        P("layer", None, "feat"),
        P("layer", "feat"),
        P("layer", None, "feat"),
        P("layer", "feat", None),
        P("layer", "feat"),
        P("layer", None, "feat"),
    )
    blocks = mesh.shape["feat"] == 8 and mesh.shape["layer"] == 4
    return jax.shard_map(
        on_device if blocks else plain,
        mesh=mesh,
        in_specs=placed,
        out_specs=(P("layer", None, "feat"), P("layer", None, "feat")),
        check_vma=False,
    )
```

```python
import functools

import jax
import jax.numpy as jnp
import numpy as np
from jax import lax
from jax.experimental import pallas as pl
from jax.experimental.pallas import tpu as pltpu
from jax.sharding import PartitionSpec as P

LAYERS = 8
GROUPS = 4
VMEM = pl.BlockSpec(memory_space=pltpu.VMEM)
SMEM = pl.BlockSpec(memory_space=pltpu.SMEM)
HBM = pl.BlockSpec(memory_space=pltpu.HBM)
SLOTS = 3
CHUNKS = 2
LIMIT = 48 * 2**20


def plain(resid, enc, enc_bias, fire, dec, dec_bias, target):
    group = lax.axis_index("layer")
    half = LAYERS // 2
    pre = jnp.einsum(
        "ltd,ldf->ltf",
        lax.all_gather(resid, "feat", axis=2, tiled=True),
        enc,
        preferred_element_type=jnp.float32,
    )
    acts = (fire.astype(jnp.float32) * (pre + enc_bias[:, None, :])).astype(jnp.bfloat16)
    every = lax.all_gather(acts, "layer", axis=0, tiled=True)
    order = jnp.arange(LAYERS + 1, dtype=jnp.int32)
    early = order <= group
    source_ids = jnp.where(early, order, order - group - 1)
    chosen = jnp.take(every, source_ids, axis=0)
    lead_mask = early[:half].astype(jnp.bfloat16)[:, None, None]
    lead_acts = chosen[:half]
    low = jnp.einsum(
        "ktf,kfd->td", lead_acts * lead_mask, dec[:half], preferred_element_type=jnp.float32
    )
    high = jnp.einsum(
        "ktf,kfd->td", lead_acts * (1 - lead_mask), dec[:half], preferred_element_type=jnp.float32
    )
    high = high + jnp.einsum(
        "ktf,kfd->td", chosen[half:], dec[half:], preferred_element_type=jnp.float32
    )
    partial_value = jnp.stack([low, high])
    recon = lax.psum(partial_value, "feat")
    whole_target, whole_bias = (
        lax.all_gather(target, "feat", axis=2, tiled=True),
        lax.all_gather(dec_bias, "feat", axis=1, tiled=True),
    )
    wide_error = (
        recon + whole_bias.astype(jnp.float32)[:, None, :] - whole_target.astype(jnp.float32)
    ).astype(jnp.bfloat16)
    columns = target.shape[2]
    error = lax.dynamic_slice_in_dim(wide_error, lax.axis_index("feat") * columns, columns, 2)
    lead_error = jnp.where(early[:half, None, None], wide_error[0][None], wide_error[1][None])
    grads_lead = jnp.einsum(
        "ktd,kfd->ktf", lead_error, dec[:half], preferred_element_type=jnp.float32
    )
    grads_rest = jnp.einsum(
        "td,kfd->ktf", wide_error[1], dec[half:], preferred_element_type=jnp.float32
    )
    pair_grads = jnp.concatenate([grads_lead, grads_rest], axis=0)
    one_hot = (source_ids[:, None] == jnp.arange(LAYERS, dtype=jnp.int32)[None, :]).astype(
        jnp.float32
    )
    grad_terms = jnp.einsum("ks,ktf->stf", one_hot, pair_grads, precision=lax.Precision.HIGHEST)
    summed = lax.psum_scatter(
        grad_terms.astype(jnp.bfloat16), "layer", scatter_dimension=0, tiled=True
    ).astype(jnp.float32)
    act_grad = fire.astype(jnp.float32) * summed
    return (error, act_grad)


ONE = [(0, 1), (1, 0), (2, 3)]
MIDDLE = [(1, 2), (2, 1)]
TWO = [(0, 2), (2, 0), (1, 3), (3, 1)]
RELAY = [(2, 3), (1, 0)]
BUFFER = [[0, 1, 3, 4], [1, 0, 2, 3], [3, 2, 0, 1], [4, 3, 1, 0]]
MIX = [(0, 1), (3, 2), (2, 0), (1, 3)]
ENDS = [(0, 3), (3, 0)]
BACK_ONE = [(0, 1), (1, 0), (3, 2)]
FLIP = [(i, i ^ 1) for i in range(8)]
FIRST = [(i, i ^ (4 if i & 1 else 2)) for i in range(8)]
SECOND = [(i, i ^ (2 if i & 1 else 4)) for i in range(8)]


def pairs_of(group):
    return [(k, k, 0) if k <= group else (k, k - group - 1, 1) for k in range(LAYERS + 1)]


def table(entries):
    out = np.zeros((GROUPS, 1 + max(len(e) for e in entries), 4), np.int32)
    for g, rows in enumerate(entries):
        out[g, 0, 0] = len(rows)
        slots = [slot for _, _, slot in rows]
        for i, row in enumerate(rows):
            out[g, i + 1] = (*row, slots.index(row[2]) == i)
    return out


def reconstruct_tables():
    early, late = [], []
    for g in range(GROUPS):
        rows = ([], [])
        for k, source, slot in pairs_of(g):
            buffer, odd = BUFFER[g][source // 2], source % 2
            if odd and buffer:
                rows[1].append((k, buffer - 1, slot))
            else:
                rows[0].append((k, 0 if odd else buffer + 1, slot))
        early.append(rows[0])
        late.append(rows[1])
    return table(early), table(late)


def gradient_tables():
    first, rest = [], []
    for g in range(GROUPS):
        rows = ([], [])
        for k, source, slot in pairs_of(g):
            place, odd = source // 2 ^ g, source % 2
            if place == 2 or (place == 3 and g < 2):
                rows[0].append((k, 2 * (place - 2) + odd, slot))
            else:
                rows[1].append((k, 2 * (1, 3, 0).index(place) + odd, slot))
        first.append(sorted(rows[0], key=lambda r: r[1]))
        rest.append(sorted(rows[1], key=lambda r: r[1]))
    return table(first), table(rest)


def bring(sources, places, sems):
    copies = [
        pltpu.make_async_copy(source, place, sems.at[i])
        for i, (source, place) in enumerate(zip(sources, places))
    ]
    for copy in copies:
        copy.start()
    return copies


def encode_kernel(layer, order, bias, *refs):
    *blocks, enc, fire, out, held, weight, mask, acc, sems, wsems, fsem = refs
    width = blocks[0].shape[1]
    rows = [pl.ds(pl.multiple_of(order[i] * width, width), width) for i in range(8)]
    weights = bring([enc.at[layer, r, :] for r in rows], [weight.at[i] for i in range(8)], wsems)
    values = bring(blocks, [held.at[i] for i in range(8)], sems)
    fired = pltpu.make_async_copy(fire.at[layer], mask, fsem)
    fired.start()
    for i in range(8):
        values[i].wait()
        weights[i].wait()
        term = jnp.dot(held[i], weight[i], preferred_element_type=jnp.float32)
        if i == 0:
            acc[...] = term
        else:
            acc[...] += term
    fired.wait()
    value = acc[...] + bias[layer : layer + 1, :]
    out[...] = (mask[...].astype(jnp.float32) * value).astype(jnp.bfloat16)


def encode(order, blocks, enc, bias, fire, layer):
    tokens, width = blocks[0].shape
    _, depth, feats = enc.shape
    return pl.pallas_call(
        functools.partial(encode_kernel, layer),
        in_specs=[SMEM, VMEM] + [HBM] * 10,
        out_specs=VMEM,
        out_shape=jax.ShapeDtypeStruct((tokens, feats), jnp.bfloat16),
        scratch_shapes=[
            pltpu.VMEM((8, tokens, width), jnp.bfloat16),
            pltpu.VMEM((8, width, feats), jnp.bfloat16),
            pltpu.VMEM((tokens, feats), jnp.int32),
            pltpu.VMEM((tokens, feats), jnp.float32),
            pltpu.SemaphoreType.DMA((8,)),
            pltpu.SemaphoreType.DMA((8,)),
            pltpu.SemaphoreType.DMA(()),
        ],
        compiler_params=pltpu.CompilerParams(vmem_limit_bytes=LIMIT),
        cost_estimate=cost(1),
        name="encode",
    )(order, bias, *blocks, enc, fire)


def fetch(entries, dec, ring, sems, i):
    slot = i % SLOTS
    return pltpu.make_async_copy(dec.at[entries[i + 1, 0]], ring.at[slot], sems.at[slot])


def open_stream(entries, dec, ring, sems):
    for i in range(SLOTS):

        @pl.when(i < entries[0, 0])
        def _():
            fetch(entries, dec, ring, sems, i).start()


def run_stream(entries, dec, ring, sems, use):
    count = entries[0, 0]

    def step(i, carry):
        fetch(entries, dec, ring, sems, i).wait()
        use(i + 1, ring.at[i % SLOTS])

        @pl.when(i + SLOTS < count)
        def _():
            fetch(entries, dec, ring, sems, i + SLOTS).start()

        return carry

    lax.fori_loop(0, count, step, 0)


def stream_scratch(dec):
    return [pltpu.VMEM((SLOTS, *dec.shape[1:]), dec.dtype), pltpu.SemaphoreType.DMA((SLOTS,))]


def cost(weight):
    return pl.CostEstimate(flops=weight * 10**9, bytes_accessed=weight * 2**20, transcendentals=0)


def add_pair(acc, slot, acts, dec):
    quarter = dec.shape[1] // 4
    for j in range(4):
        part = slice(j * quarter, (j + 1) * quarter)
        acc[slot, :, part] += jnp.dot(acts, dec[:, part], preferred_element_type=jnp.float32)


def early_kernel(entries, *refs):
    *sources, dec, out, held, acc, hsems, ring, sems = refs
    copies = bring(sources, [held.at[i] for i in range(len(sources))], hsems)
    open_stream(entries, dec, ring, sems)
    acc[...] = jnp.zeros_like(acc)
    for copy in copies:
        copy.wait()

    def use(e, block):
        add_pair(acc, entries[e, 2], held[entries[e, 1]], block)

    run_stream(entries, dec, ring, sems, use)
    out[...] = acc[...].astype(out.dtype)


def reconstruct_early(entries, sources, dec):
    tokens, feats = sources[0].shape
    depth = dec.shape[2]
    return pl.pallas_call(
        early_kernel,
        in_specs=[SMEM] + [HBM] * len(sources) + [HBM],
        out_specs=VMEM,
        scratch_shapes=[
            pltpu.VMEM((len(sources), tokens, feats), jnp.bfloat16),
            pltpu.VMEM((2, tokens, depth), jnp.float32),
            pltpu.SemaphoreType.DMA((len(sources),)),
        ]
        + stream_scratch(dec),
        out_shape=jax.ShapeDtypeStruct((2, tokens, depth), jnp.bfloat16),
        compiler_params=pltpu.CompilerParams(vmem_limit_bytes=LIMIT),
        cost_estimate=cost(10),
        name="reconstruct_early",
    )(entries, *sources, dec)


def late_kernel(entries, cols, *refs):
    *sources, before, dec, keep0, send0, keep1, send1, held, acc, earlier, hsems, ring, sems = refs
    copies = bring([*sources, before], [held.at[i] for i in range(len(sources))] + [earlier], hsems)
    open_stream(entries, dec, ring, sems)
    acc[...] = jnp.zeros_like(acc)
    tokens, width = keep0.shape[2:]
    for copy in copies[:-1]:
        copy.wait()

    def use(e, block):
        add_pair(acc, entries[e, 2], held[entries[e, 1]], block)

    run_stream(entries, dec, ring, sems, use)
    copies[-1].wait()
    for c, (keep, send) in enumerate(((keep0, send0), (keep1, send1))):
        rows = slice(c * tokens, (c + 1) * tokens)
        for i in range(8):
            place = pl.ds(pl.multiple_of(cols[i] * width, width), width)
            out = keep if i < 4 else send
            for s in range(2):
                value = acc[s, rows, place] + earlier[s, rows, place].astype(jnp.float32)
                out[i % 4, s] = value.astype(jnp.bfloat16)


def reconstruct_late(entries, cols, sources, before, dec):
    tokens, feats = sources[0].shape
    depth = dec.shape[2]
    out = jax.ShapeDtypeStruct((4, 2, tokens // CHUNKS, depth // 8), jnp.bfloat16)
    return pl.pallas_call(
        late_kernel,
        in_specs=[SMEM] * 2 + [HBM] * len(sources) + [HBM, HBM],
        out_specs=[VMEM] * 4,
        scratch_shapes=[
            pltpu.VMEM((len(sources), tokens, feats), jnp.bfloat16),
            pltpu.VMEM((2, tokens, depth), jnp.float32),
            pltpu.VMEM((2, tokens, depth), jnp.bfloat16),
            pltpu.SemaphoreType.DMA((len(sources) + 1,)),
        ]
        + stream_scratch(dec),
        out_shape=[out] * 4,
        compiler_params=pltpu.CompilerParams(vmem_limit_bytes=LIMIT),
        cost_estimate=cost(10),
        name="reconstruct_late",
    )(entries, cols, *sources, before, dec)


def add_term(entries, e, error, total, block):
    total[entries[e, 1]] += lax.dot_general(
        error[entries[e, 2]], block[...], (((1,), (1,)), ((), ())), preferred_element_type=jnp.float32
    )


def first_kernel(entries, cols, *refs):
    *blocks, dec, two, three, error, total, bsems, ring, sems = refs
    tokens, width = blocks[0].shape[1:]
    places = [pl.ds(pl.multiple_of(cols[j] * width, width), width) for j in range(8)]
    copies = bring(
        blocks,
        [error.at[:, c * tokens : (c + 1) * tokens, p] for c in range(len(blocks) // 8) for p in places],
        bsems,
    )
    open_stream(entries, dec, ring, sems)
    total[...] = jnp.zeros_like(total)
    for copy in copies:
        copy.wait()
    run_stream(
        entries, dec, ring, sems, lambda e, block: add_term(entries, e, error, total, block)
    )
    two[...] = total[:2].astype(two.dtype)
    three[...] = total[2:]


def first_gradients(entries, cols, blocks, dec):
    tokens = blocks[0].shape[1] * (len(blocks) // 8)
    _, feats, depth = dec.shape
    return pl.pallas_call(
        first_kernel,
        in_specs=[SMEM] * 2 + [HBM] * len(blocks) + [HBM],
        out_specs=[VMEM] * 3,
        scratch_shapes=[
            pltpu.VMEM((4, tokens, feats), jnp.float32),
            pltpu.SemaphoreType.DMA((len(blocks),)),
        ]
        + stream_scratch(dec),
        out_shape=[
            jax.ShapeDtypeStruct((2, tokens, feats), jnp.bfloat16),
            jax.ShapeDtypeStruct((2, tokens, feats), jnp.float32),
            jax.ShapeDtypeStruct((2, tokens, depth), jnp.bfloat16),
        ],
        compiler_params=pltpu.CompilerParams(vmem_limit_bytes=LIMIT),
        cost_estimate=cost(10),
        name="first_gradients",
    )(entries, cols, *blocks, dec)


def rest_kernel(entries, whole, begun, dec, one, three, own, error, total, esem, tsem, ring, sems):
    copy = pltpu.make_async_copy(whole, error, esem)
    copy.start()
    more = pltpu.make_async_copy(begun, total.at[2:4], tsem)
    more.start()
    open_stream(entries, dec, ring, sems)
    total[0:2] = jnp.zeros_like(total[0:2])
    total[4:6] = jnp.zeros_like(total[4:6])
    copy.wait()
    more.wait()
    run_stream(
        entries, dec, ring, sems, lambda e, block: add_term(entries, e, error, total, block)
    )
    for i, out in enumerate((one, three, own)):
        out[...] = total[2 * i : 2 * i + 2].astype(out.dtype)


def rest_gradients(entries, whole, begun, dec):
    _, tokens, depth = whole.shape
    feats = dec.shape[1]
    return pl.pallas_call(
        rest_kernel,
        in_specs=[SMEM, HBM, HBM, HBM],
        out_specs=[VMEM] * 3,
        scratch_shapes=[
            pltpu.VMEM((2, tokens, depth), jnp.bfloat16),
            pltpu.VMEM((6, tokens, feats), jnp.float32),
            pltpu.SemaphoreType.DMA(()),
            pltpu.SemaphoreType.DMA(()),
        ]
        + stream_scratch(dec),
        out_shape=[
            jax.ShapeDtypeStruct((2, tokens, feats), t)
            for t in (jnp.bfloat16, jnp.bfloat16, jnp.float32)
        ],
        compiler_params=pltpu.CompilerParams(vmem_limit_bytes=LIMIT),
        cost_estimate=cost(10),
        name="rest_gradients",
    )(entries, whole, begun, dec)


def gather(own):
    first = lax.ppermute(own, "feat", FIRST)
    second = lax.ppermute(own, "feat", SECOND)
    both = lax.ppermute(first, "feat", SECOND)
    mine = [own, first, second, both]
    return mine + [lax.ppermute(b, "feat", FLIP) for b in mine]


def on_device(resid, enc, enc_bias, fire, dec, dec_bias, target):
    f32, bf16 = jnp.float32, jnp.bfloat16
    group = lax.axis_index("layer")
    me = lax.axis_index("feat")
    core = me & 1
    one, two = 2 + 2 * core, 4 - 2 * core
    none = 0 * core
    near = jnp.stack([none, one, two, none + 6, none + 1, two ^ 1, one ^ 1, none + 7])
    columns = (me ^ near).astype(jnp.int32)
    early_table, late_table = (jnp.asarray(t)[group] for t in reconstruct_tables())
    first_table, rest_table = (jnp.asarray(t)[group] for t in gradient_tables())

    masks = pltpu.with_memory_space_constraint(fire, pltpu.HBM)
    ways = []
    for layer in range(2):
        acts = encode(columns, gather(resid[layer]), enc, enc_bias, masks, layer)
        two_away = lax.ppermute(acts, "layer", TWO)
        nearest = lax.ppermute(acts, "layer", ONE)
        middle = lax.ppermute(acts, "layer", MIDDLE)
        relayed = lax.ppermute(two_away, "layer", RELAY)
        ways.append((acts, nearest, middle, two_away, relayed))
    a, b = ways
    before = reconstruct_early(early_table, [b[0], *a], dec)
    halves = reconstruct_late(late_table, columns, b[1:], before, dec)

    tokens = resid.shape[1] // CHUNKS
    errors, blocks = [], []
    for c in range(CHUNKS):
        span = slice(c * tokens, (c + 1) * tokens)
        keep, send = halves[2 * c : 2 * c + 2]
        pair = keep.astype(f32) + lax.ppermute(send, "feat", FLIP).astype(f32)
        far = lax.ppermute(pair[2:].astype(bf16), "feat", SECOND).astype(f32)
        close = lax.ppermute((pair[1] + far[1]).astype(bf16), "feat", FIRST).astype(f32)
        recon = pair[0] + far[0] + close
        error = recon + dec_bias.astype(f32)[:, None, :] - target[:, span].astype(f32)
        errors.append(error.astype(bf16))
        blocks += gather(errors[c])

    two_away, begun, whole = first_gradients(first_table, columns, blocks, dec)
    mixed = lax.ppermute(two_away, "layer", MIX)
    one_away, three_away, own = rest_gradients(rest_table, whole, begun, dec)
    ends = lax.ppermute(three_away, "layer", ENDS)
    middle = (three_away.astype(f32) + mixed.astype(f32)).astype(bf16)
    middle = lax.ppermute(middle, "layer", MIDDLE)
    one_away = lax.ppermute(one_away, "layer", BACK_ONE)
    inner = (group == 1) | (group == 2)
    total = own + one_away.astype(f32) + middle.astype(f32)
    total = total + jnp.where(inner, 0.0, mixed.astype(f32) + ends.astype(f32))
    return jnp.concatenate(errors, axis=1), fire.astype(f32) * total


def solution(mesh):
    placed = (
        P("layer", None, "feat"),
        P("layer", None, "feat"),
        P("layer", "feat"),
        P("layer", None, "feat"),
        P("layer", "feat", None),
        P("layer", "feat"),
        P("layer", None, "feat"),
    )
    blocks = mesh.shape["feat"] == 8 and mesh.shape["layer"] == GROUPS
    return jax.shard_map(
        on_device if blocks else plain,
        mesh=mesh,
        in_specs=placed,
        out_specs=(P("layer", None, "feat"), P("layer", None, "feat")),
        check_vma=False,
    )
```

```python
import functools

import jax
import jax.numpy as jnp
import numpy as np
from jax import lax
from jax.experimental import pallas as pl
from jax.experimental.pallas import tpu as pltpu
from jax.sharding import PartitionSpec as P

LAYERS = 8
GROUPS = 4
VMEM = pl.BlockSpec(memory_space=pltpu.VMEM)
SMEM = pl.BlockSpec(memory_space=pltpu.SMEM)
HBM = pl.BlockSpec(memory_space=pltpu.HBM)
SLOTS = 3
CHUNKS = 2
LIMIT = 32 * 2**20


def plain(resid, enc, enc_bias, fire, dec, dec_bias, target):
    group = lax.axis_index("layer")
    half = LAYERS // 2
    pre = jnp.einsum(
        "ltd,ldf->ltf",
        lax.all_gather(resid, "feat", axis=2, tiled=True),
        enc,
        preferred_element_type=jnp.float32,
    )
    acts = (fire.astype(jnp.float32) * (pre + enc_bias[:, None, :])).astype(jnp.bfloat16)
    every = lax.all_gather(acts, "layer", axis=0, tiled=True)
    order = jnp.arange(LAYERS + 1, dtype=jnp.int32)
    early = order <= group
    source_ids = jnp.where(early, order, order - group - 1)
    chosen = jnp.take(every, source_ids, axis=0)
    lead_mask = early[:half].astype(jnp.bfloat16)[:, None, None]
    lead_acts = chosen[:half]
    low = jnp.einsum(
        "ktf,kfd->td", lead_acts * lead_mask, dec[:half], preferred_element_type=jnp.float32
    )
    high = jnp.einsum(
        "ktf,kfd->td", lead_acts * (1 - lead_mask), dec[:half], preferred_element_type=jnp.float32
    )
    high = high + jnp.einsum(
        "ktf,kfd->td", chosen[half:], dec[half:], preferred_element_type=jnp.float32
    )
    partial_value = jnp.stack([low, high])
    recon = lax.psum(partial_value, "feat")
    whole_target, whole_bias = (
        lax.all_gather(target, "feat", axis=2, tiled=True),
        lax.all_gather(dec_bias, "feat", axis=1, tiled=True),
    )
    wide_error = (
        recon + whole_bias.astype(jnp.float32)[:, None, :] - whole_target.astype(jnp.float32)
    ).astype(jnp.bfloat16)
    columns = target.shape[2]
    error = lax.dynamic_slice_in_dim(wide_error, lax.axis_index("feat") * columns, columns, 2)
    lead_error = jnp.where(early[:half, None, None], wide_error[0][None], wide_error[1][None])
    grads_lead = jnp.einsum(
        "ktd,kfd->ktf", lead_error, dec[:half], preferred_element_type=jnp.float32
    )
    grads_rest = jnp.einsum(
        "td,kfd->ktf", wide_error[1], dec[half:], preferred_element_type=jnp.float32
    )
    pair_grads = jnp.concatenate([grads_lead, grads_rest], axis=0)
    one_hot = (source_ids[:, None] == jnp.arange(LAYERS, dtype=jnp.int32)[None, :]).astype(
        jnp.float32
    )
    grad_terms = jnp.einsum("ks,ktf->stf", one_hot, pair_grads, precision=lax.Precision.HIGHEST)
    summed = lax.psum_scatter(
        grad_terms.astype(jnp.bfloat16), "layer", scatter_dimension=0, tiled=True
    ).astype(jnp.float32)
    act_grad = fire.astype(jnp.float32) * summed
    return (error, act_grad)


ONE = [(0, 1), (1, 0), (2, 3)]
MIDDLE = [(1, 2), (2, 1)]
TWO = [(0, 2), (2, 0), (1, 3), (3, 1)]
RELAY = [(2, 3), (1, 0)]
BUFFER = [[0, 1, 3, 4], [1, 0, 2, 3], [3, 2, 0, 1], [4, 3, 1, 0]]
MIX = [(0, 1), (3, 2), (2, 0), (1, 3)]
ENDS = [(0, 3), (3, 0)]
BACK_ONE = [(0, 1), (1, 0), (3, 2)]
FLIP = [(i, i ^ 1) for i in range(8)]
FIRST = [(i, i ^ (4 if i & 1 else 2)) for i in range(8)]
SECOND = [(i, i ^ (2 if i & 1 else 4)) for i in range(8)]


def pairs_of(group):
    return [(k, k, 0) if k <= group else (k, k - group - 1, 1) for k in range(LAYERS + 1)]


def table(entries):
    out = np.zeros((GROUPS, 1 + max(len(e) for e in entries), 4), np.int32)
    for g, rows in enumerate(entries):
        out[g, 0, 0] = len(rows)
        slots = [slot for _, _, slot in rows]
        for i, row in enumerate(rows):
            out[g, i + 1] = (*row, slots.index(row[2]) == i)
    return out


def reconstruct_tables():
    early, late = [], []
    for g in range(GROUPS):
        rows = ([], [])
        for k, source, slot in pairs_of(g):
            buffer, odd = BUFFER[g][source // 2], source % 2
            if odd and buffer:
                rows[1].append((k, buffer - 1, slot))
            elif buffer == 4:
                rows[1].append((k, 4, slot))
            else:
                rows[0].append((k, 0 if odd else buffer + 1, slot))
        early.append(rows[0])
        late.append(rows[1])
    return table(early), table(late)


def gradient_tables():
    first, rest, last = [], [], []
    for g in range(GROUPS):
        rows = ([], [], [])
        for k, source, slot in pairs_of(g):
            place, odd = source // 2 ^ g, source % 2
            if place == 0:
                rows[2].append((k, odd, slot))
            elif place == 2 or (place == 3 and g < 2):
                rows[0].append((k, 2 * (place - 2) + odd, slot))
            else:
                rows[1].append((k, place - 1 + odd, slot))
        first.append(sorted(rows[0], key=lambda r: r[1]))
        rest.append(sorted(rows[1], key=lambda r: r[1]))
        last.append(sorted(rows[2], key=lambda r: r[1]))
    return table(first), table(rest), table(last)


def bring(sources, places, sems):
    copies = [
        pltpu.make_async_copy(source, place, sems.at[i])
        for i, (source, place) in enumerate(zip(sources, places))
    ]
    for copy in copies:
        copy.start()
    return copies


def encode_kernel(layer, order, *refs):
    *blocks, bias, enc, fire, out, held, weight, mask, shift, acc, sems, wsems, fsem, ssem = refs
    width = blocks[0].shape[1]
    rows = [pl.ds(pl.multiple_of(order[i] * width, width), width) for i in range(8)]
    weights = bring([enc.at[layer, r, :] for r in rows], [weight.at[i] for i in range(8)], wsems)
    values = bring(blocks, [held.at[i] for i in range(8)], sems)
    fired = pltpu.make_async_copy(fire.at[layer], mask, fsem)
    fired.start()
    shifted = pltpu.make_async_copy(bias, shift, ssem)
    shifted.start()
    for i in range(8):
        values[i].wait()
        weights[i].wait()
        term = jnp.dot(held[i], weight[i], preferred_element_type=jnp.float32)
        if i == 0:
            acc[...] = term
        else:
            acc[...] += term
    fired.wait()
    shifted.wait()
    value = acc[...] + shift[layer : layer + 1, :]
    out[...] = (mask[...].astype(jnp.float32) * value).astype(jnp.bfloat16)


def encode(order, blocks, enc, bias, fire, layer):
    tokens, width = blocks[0].shape
    _, depth, feats = enc.shape
    return pl.pallas_call(
        functools.partial(encode_kernel, layer),
        in_specs=[SMEM] + [HBM] * 11,
        out_specs=VMEM,
        out_shape=jax.ShapeDtypeStruct((tokens, feats), jnp.bfloat16),
        scratch_shapes=[
            pltpu.VMEM((8, tokens, width), jnp.bfloat16),
            pltpu.VMEM((8, width, feats), jnp.bfloat16),
            pltpu.VMEM((tokens, feats), jnp.int32),
            pltpu.VMEM(bias.shape, jnp.float32),
            pltpu.VMEM((tokens, feats), jnp.float32),
            pltpu.SemaphoreType.DMA((8,)),
            pltpu.SemaphoreType.DMA((8,)),
            pltpu.SemaphoreType.DMA(()),
            pltpu.SemaphoreType.DMA(()),
        ],
        compiler_params=pltpu.CompilerParams(vmem_limit_bytes=LIMIT),
        cost_estimate=cost(1),
        name="encode",
    )(order, *blocks, bias, enc, fire)


def fetch(entries, dec, ring, sems, i):
    slot = i % SLOTS
    return pltpu.make_async_copy(dec.at[entries[i + 1, 0]], ring.at[slot], sems.at[slot])


def open_stream(entries, dec, ring, sems):
    for i in range(SLOTS):

        @pl.when(i < entries[0, 0])
        def _():
            fetch(entries, dec, ring, sems, i).start()


def run_stream(entries, dec, ring, sems, use):
    count = entries[0, 0]

    def step(i, carry):
        fetch(entries, dec, ring, sems, i).wait()
        use(i + 1, ring.at[i % SLOTS])

        @pl.when(i + SLOTS < count)
        def _():
            fetch(entries, dec, ring, sems, i + SLOTS).start()

        return carry

    lax.fori_loop(0, count, step, 0)


def stream_scratch(dec):
    return [pltpu.VMEM((SLOTS, *dec.shape[1:]), dec.dtype), pltpu.SemaphoreType.DMA((SLOTS,))]


def cost(weight):
    return pl.CostEstimate(flops=weight * 10**9, bytes_accessed=weight * 2**20, transcendentals=0)


def add_pair(acc, slot, acts, dec):
    quarter = dec.shape[1] // 4
    for j in range(4):
        part = slice(j * quarter, (j + 1) * quarter)
        acc[slot, :, part] += jnp.dot(acts, dec[:, part], preferred_element_type=jnp.float32)


def early_kernel(entries, *refs):
    *sources, dec, out, held, acc, hsems, ring, sems = refs
    copies = bring(sources, [held.at[i] for i in range(len(sources))], hsems)
    open_stream(entries, dec, ring, sems)
    acc[...] = jnp.zeros_like(acc)
    for copy in copies:
        copy.wait()

    def use(e, block):
        add_pair(acc, entries[e, 2], held[entries[e, 1]], block)

    run_stream(entries, dec, ring, sems, use)
    out[...] = acc[...].astype(out.dtype)


def reconstruct_early(entries, sources, dec):
    tokens, feats = sources[0].shape
    depth = dec.shape[2]
    return pl.pallas_call(
        early_kernel,
        in_specs=[SMEM] + [HBM] * len(sources) + [HBM],
        out_specs=VMEM,
        scratch_shapes=[
            pltpu.VMEM((len(sources), tokens, feats), jnp.bfloat16),
            pltpu.VMEM((2, tokens, depth), jnp.float32),
            pltpu.SemaphoreType.DMA((len(sources),)),
        ]
        + stream_scratch(dec),
        out_shape=jax.ShapeDtypeStruct((2, tokens, depth), jnp.bfloat16),
        compiler_params=pltpu.CompilerParams(vmem_limit_bytes=LIMIT),
        cost_estimate=cost(10),
        name="reconstruct_early",
    )(entries, *sources, dec)


def late_kernel(entries, cols, *refs):
    *sources, before, dec, keep0, send0, keep1, send1, held, acc, earlier, hsems, ring, sems = refs
    copies = bring([*sources, before], [held.at[i] for i in range(len(sources))] + [earlier], hsems)
    open_stream(entries, dec, ring, sems)
    acc[...] = jnp.zeros_like(acc)
    tokens, width = keep0.shape[2:]
    for copy in copies[:-1]:
        copy.wait()

    def use(e, block):
        add_pair(acc, entries[e, 2], held[entries[e, 1]], block)

    run_stream(entries, dec, ring, sems, use)
    copies[-1].wait()
    for c, (keep, send) in enumerate(((keep0, send0), (keep1, send1))):
        rows = slice(c * tokens, (c + 1) * tokens)
        for i in range(8):
            place = pl.ds(pl.multiple_of(cols[i] * width, width), width)
            out = keep if i < 4 else send
            for s in range(2):
                value = acc[s, rows, place] + earlier[s, rows, place].astype(jnp.float32)
                out[i % 4, s] = value.astype(jnp.bfloat16)


def reconstruct_late(entries, cols, sources, before, dec):
    tokens, feats = sources[0].shape
    depth = dec.shape[2]
    out = jax.ShapeDtypeStruct((4, 2, tokens // CHUNKS, depth // 8), jnp.bfloat16)
    return pl.pallas_call(
        late_kernel,
        in_specs=[SMEM] * 2 + [HBM] * len(sources) + [HBM, HBM],
        out_specs=[VMEM] * 4,
        scratch_shapes=[
            pltpu.VMEM((len(sources), tokens, feats), jnp.bfloat16),
            pltpu.VMEM((2, tokens, depth), jnp.float32),
            pltpu.VMEM((2, tokens, depth), jnp.bfloat16),
            pltpu.SemaphoreType.DMA((len(sources) + 1,)),
        ]
        + stream_scratch(dec),
        out_shape=[out] * 4,
        compiler_params=pltpu.CompilerParams(vmem_limit_bytes=LIMIT),
        cost_estimate=cost(10),
        name="reconstruct_late",
    )(entries, cols, *sources, before, dec)


def add_term(entries, e, error, total, block):
    total[entries[e, 1]] += lax.dot_general(
        error[entries[e, 2]], block[...], (((1,), (1,)), ((), ())), preferred_element_type=jnp.float32
    )


def first_kernel(entries, cols, *refs):
    *blocks, dec, two, three, error, total, bsems, ring, sems = refs
    tokens, width = blocks[0].shape[1:]
    places = [pl.ds(pl.multiple_of(cols[j] * width, width), width) for j in range(8)]
    copies = bring(
        blocks,
        [error.at[:, c * tokens : (c + 1) * tokens, p] for c in range(len(blocks) // 8) for p in places],
        bsems,
    )
    open_stream(entries, dec, ring, sems)
    total[...] = jnp.zeros_like(total)
    for copy in copies:
        copy.wait()
    run_stream(
        entries, dec, ring, sems, lambda e, block: add_term(entries, e, error, total, block)
    )
    two[...] = total[:2].astype(two.dtype)
    three[...] = total[2:]


def first_gradients(entries, cols, blocks, dec):
    tokens = blocks[0].shape[1] * (len(blocks) // 8)
    _, feats, depth = dec.shape
    return pl.pallas_call(
        first_kernel,
        in_specs=[SMEM] * 2 + [HBM] * len(blocks) + [HBM],
        out_specs=[VMEM] * 3,
        scratch_shapes=[
            pltpu.VMEM((4, tokens, feats), jnp.float32),
            pltpu.SemaphoreType.DMA((len(blocks),)),
        ]
        + stream_scratch(dec),
        out_shape=[
            jax.ShapeDtypeStruct((2, tokens, feats), jnp.bfloat16),
            jax.ShapeDtypeStruct((2, tokens, feats), jnp.float32),
            jax.ShapeDtypeStruct((2, tokens, depth), jnp.bfloat16),
        ],
        compiler_params=pltpu.CompilerParams(vmem_limit_bytes=LIMIT),
        cost_estimate=cost(10),
        name="first_gradients",
    )(entries, cols, *blocks, dec)


def rest_kernel(entries, whole, begun, dec, one, three, error, total, esem, tsem, ring, sems):
    copy = pltpu.make_async_copy(whole, error, esem)
    copy.start()
    more = pltpu.make_async_copy(begun, total.at[2:4], tsem)
    more.start()
    open_stream(entries, dec, ring, sems)
    total[0:2] = jnp.zeros_like(total[0:2])
    copy.wait()
    more.wait()
    run_stream(
        entries, dec, ring, sems, lambda e, block: add_term(entries, e, error, total, block)
    )
    one[...] = total[:2].astype(one.dtype)
    three[...] = total[2:].astype(three.dtype)


def rest_gradients(entries, whole, begun, dec):
    _, tokens, depth = whole.shape
    feats = dec.shape[1]
    return pl.pallas_call(
        rest_kernel,
        in_specs=[SMEM, HBM, HBM, HBM],
        out_specs=[VMEM] * 2,
        scratch_shapes=[
            pltpu.VMEM((2, tokens, depth), jnp.bfloat16),
            pltpu.VMEM((4, tokens, feats), jnp.float32),
            pltpu.SemaphoreType.DMA(()),
            pltpu.SemaphoreType.DMA(()),
        ]
        + stream_scratch(dec),
        out_shape=[jax.ShapeDtypeStruct((2, tokens, feats), jnp.bfloat16)] * 2,
        compiler_params=pltpu.CompilerParams(vmem_limit_bytes=LIMIT),
        cost_estimate=cost(10),
        name="rest_gradients",
    )(entries, whole, begun, dec)


def own_kernel(entries, whole, dec, total, error, esem, ring, sems):
    copy = pltpu.make_async_copy(whole, error, esem)
    copy.start()
    open_stream(entries, dec, ring, sems)
    total[...] = jnp.zeros_like(total)
    copy.wait()
    run_stream(
        entries, dec, ring, sems, lambda e, block: add_term(entries, e, error, total, block)
    )


def own_gradients(entries, whole, dec):
    _, tokens, depth = whole.shape
    feats = dec.shape[1]
    return pl.pallas_call(
        own_kernel,
        in_specs=[SMEM, HBM, HBM],
        out_specs=VMEM,
        scratch_shapes=[pltpu.VMEM((2, tokens, depth), jnp.bfloat16), pltpu.SemaphoreType.DMA(())]
        + stream_scratch(dec),
        out_shape=jax.ShapeDtypeStruct((2, tokens, feats), jnp.float32),
        compiler_params=pltpu.CompilerParams(vmem_limit_bytes=LIMIT),
        cost_estimate=cost(10),
        name="own_gradients",
    )(entries, whole, dec)


def after(array, *others):
    return lax.optimization_barrier((array, *others))[0]


def gather(own):
    first = lax.ppermute(own, "feat", FIRST)
    second = lax.ppermute(own, "feat", SECOND)
    both = lax.ppermute(first, "feat", SECOND)
    mine = [own, first, second, both]
    return [*mine, *(lax.ppermute(b, "feat", FLIP) for b in mine)]


def on_device(resid, enc, enc_bias, fire, dec, dec_bias, target):
    f32, bf16 = jnp.float32, jnp.bfloat16
    group = lax.axis_index("layer")
    me = lax.axis_index("feat")
    core = me & 1
    one, two = 2 + 2 * core, 4 - 2 * core
    none = 0 * core
    near = jnp.stack([none, one, two, none + 6, none + 1, two ^ 1, one ^ 1, none + 7])
    columns = (me ^ near).astype(jnp.int32)
    early_table, late_table = (jnp.asarray(t)[group] for t in reconstruct_tables())
    first_table, rest_table, own_table = (jnp.asarray(t)[group] for t in gradient_tables())

    enc, enc_bias, masks = (
        pltpu.with_memory_space_constraint(x, pltpu.HBM) for x in (enc, enc_bias, fire)
    )
    ways = []
    for layer in range(2):
        acts = encode(columns, gather(resid[layer]), enc, enc_bias, masks, layer)
        two_away = lax.ppermute(acts, "layer", TWO)
        nearest = lax.ppermute(acts, "layer", ONE)
        middle = lax.ppermute(acts, "layer", MIDDLE)
        relayed = lax.ppermute(two_away, "layer", RELAY)
        ways.append((acts, nearest, middle, two_away, relayed))
    a, b = ways
    before = reconstruct_early(early_table, [b[0], *a[:4]], dec)
    halves = reconstruct_late(late_table, columns, [*b[1:], a[4]], before, dec)

    tokens = resid.shape[1] // CHUNKS
    errors, blocks = [], []
    for c in range(CHUNKS):
        span = slice(c * tokens, (c + 1) * tokens)
        keep, send = halves[2 * c : 2 * c + 2]
        pair = keep.astype(f32) + lax.ppermute(send, "feat", FLIP).astype(f32)
        far = lax.ppermute(pair[2:].astype(bf16), "feat", SECOND).astype(f32)
        close = (pair[1] + far[1]).astype(bf16)
        if errors:
            close = after(close, errors[0])
        close = lax.ppermute(close, "feat", FIRST).astype(f32)
        recon = pair[0] + far[0] + close
        error = recon + dec_bias.astype(f32)[:, None, :] - target[:, span].astype(f32)
        errors.append(error.astype(bf16))
        blocks += gather(errors[c])

    two_away, begun, whole = first_gradients(first_table, columns, blocks, dec)
    mixed = lax.ppermute(two_away, "layer", MIX)
    one_away, three_away = rest_gradients(rest_table, whole, begun, dec)
    ends = lax.ppermute(three_away, "layer", ENDS)
    across = (three_away.astype(f32) + mixed.astype(f32)).astype(bf16)
    middle = lax.ppermute(across, "layer", MIDDLE)
    back = lax.ppermute(one_away, "layer", BACK_ONE)
    own = own_gradients(after(own_table, across), whole, dec)
    inner = (group == 1) | (group == 2)
    here = after(own + jnp.where(inner, 0.0, mixed.astype(f32)))
    total = here + back.astype(f32) + middle.astype(f32) + ends.astype(f32)
    errors[0] = after(errors[0], one_away)
    return jnp.concatenate(errors, axis=1), fire.astype(f32) * total


def solution(mesh):
    placed = (
        P("layer", None, "feat"),
        P("layer", None, "feat"),
        P("layer", "feat"),
        P("layer", None, "feat"),
        P("layer", "feat", None),
        P("layer", "feat"),
        P("layer", None, "feat"),
    )
    blocks = mesh.shape["feat"] == 8 and mesh.shape["layer"] == GROUPS
    return jax.shard_map(
        on_device if blocks else plain,
        mesh=mesh,
        in_specs=placed,
        out_specs=(P("layer", None, "feat"), P("layer", None, "feat")),
        check_vma=False,
    )
```

```python
import functools

import jax
import jax.numpy as jnp
import numpy as np
from jax import lax
from jax.experimental import pallas as pl
from jax.experimental.pallas import tpu as pltpu
from jax.sharding import PartitionSpec as P

LAYERS = 8
GROUPS = 4
VMEM = pl.BlockSpec(memory_space=pltpu.VMEM)
SMEM = pl.BlockSpec(memory_space=pltpu.SMEM)
HBM = pl.BlockSpec(memory_space=pltpu.HBM)
SLOTS = 3
CHUNKS = 2
LIMIT = 32 * 2**20


def plain(resid, enc, enc_bias, fire, dec, dec_bias, target):
    group = lax.axis_index("layer")
    half = LAYERS // 2
    pre = jnp.einsum(
        "ltd,ldf->ltf",
        lax.all_gather(resid, "feat", axis=2, tiled=True),
        enc,
        preferred_element_type=jnp.float32,
    )
    acts = (fire.astype(jnp.float32) * (pre + enc_bias[:, None, :])).astype(jnp.bfloat16)
    every = lax.all_gather(acts, "layer", axis=0, tiled=True)
    order = jnp.arange(LAYERS + 1, dtype=jnp.int32)
    early = order <= group
    source_ids = jnp.where(early, order, order - group - 1)
    chosen = jnp.take(every, source_ids, axis=0)
    lead_mask = early[:half].astype(jnp.bfloat16)[:, None, None]
    lead_acts = chosen[:half]
    low = jnp.einsum(
        "ktf,kfd->td", lead_acts * lead_mask, dec[:half], preferred_element_type=jnp.float32
    )
    high = jnp.einsum(
        "ktf,kfd->td", lead_acts * (1 - lead_mask), dec[:half], preferred_element_type=jnp.float32
    )
    high = high + jnp.einsum(
        "ktf,kfd->td", chosen[half:], dec[half:], preferred_element_type=jnp.float32
    )
    partial_value = jnp.stack([low, high])
    recon = lax.psum(partial_value, "feat")
    whole_target, whole_bias = (
        lax.all_gather(target, "feat", axis=2, tiled=True),
        lax.all_gather(dec_bias, "feat", axis=1, tiled=True),
    )
    wide_error = (
        recon + whole_bias.astype(jnp.float32)[:, None, :] - whole_target.astype(jnp.float32)
    ).astype(jnp.bfloat16)
    columns = target.shape[2]
    error = lax.dynamic_slice_in_dim(wide_error, lax.axis_index("feat") * columns, columns, 2)
    lead_error = jnp.where(early[:half, None, None], wide_error[0][None], wide_error[1][None])
    grads_lead = jnp.einsum(
        "ktd,kfd->ktf", lead_error, dec[:half], preferred_element_type=jnp.float32
    )
    grads_rest = jnp.einsum(
        "td,kfd->ktf", wide_error[1], dec[half:], preferred_element_type=jnp.float32
    )
    pair_grads = jnp.concatenate([grads_lead, grads_rest], axis=0)
    one_hot = (source_ids[:, None] == jnp.arange(LAYERS, dtype=jnp.int32)[None, :]).astype(
        jnp.float32
    )
    grad_terms = jnp.einsum("ks,ktf->stf", one_hot, pair_grads, precision=lax.Precision.HIGHEST)
    summed = lax.psum_scatter(
        grad_terms.astype(jnp.bfloat16), "layer", scatter_dimension=0, tiled=True
    ).astype(jnp.float32)
    act_grad = fire.astype(jnp.float32) * summed
    return (error, act_grad)


ONE = [(0, 1), (1, 0), (2, 3)]
MIDDLE = [(1, 2), (2, 1)]
TWO = [(0, 2), (2, 0), (1, 3), (3, 1)]
RELAY = [(2, 3), (1, 0)]
BUFFER = [[0, 1, 3, 4], [1, 0, 2, 3], [3, 2, 0, 1], [4, 3, 1, 0]]
MIX = [(0, 1), (3, 2), (2, 0), (1, 3)]
ENDS = [(0, 3), (3, 0)]
BACK_ONE = [(0, 1), (1, 0), (3, 2)]
FLIP = [(i, i ^ 1) for i in range(8)]
FIRST = [(i, i ^ (4 if i & 1 else 2)) for i in range(8)]
SECOND = [(i, i ^ (2 if i & 1 else 4)) for i in range(8)]


def pairs_of(group):
    return [(k, k, 0) if k <= group else (k, k - group - 1, 1) for k in range(LAYERS + 1)]


def table(entries):
    out = np.zeros((GROUPS, 1 + max(len(e) for e in entries), 4), np.int32)
    for g, rows in enumerate(entries):
        out[g, 0, 0] = len(rows)
        slots = [slot for _, _, slot in rows]
        for i, row in enumerate(rows):
            out[g, i + 1] = (*row, slots.index(row[2]) == i)
    return out


def reconstruct_tables():
    early, late = [], []
    for g in range(GROUPS):
        rows = ([], [])
        for k, source, slot in pairs_of(g):
            buffer, odd = BUFFER[g][source // 2], source % 2
            if odd and buffer:
                rows[1].append((k, buffer - 1, slot))
            elif buffer == 4:
                rows[1].append((k, 4, slot))
            else:
                rows[0].append((k, 0 if odd else buffer + 1, slot))
        early.append(rows[0])
        late.append(rows[1])
    return table(early), table(late)


def gradient_tables():
    first, rest, last = [], [], []
    for g in range(GROUPS):
        rows = ([], [], [])
        for k, source, slot in pairs_of(g):
            place, odd = source // 2 ^ g, source % 2
            if place == 0:
                rows[2].append((k, odd, slot))
            elif place == 2 or (place == 3 and g < 2):
                rows[0].append((k, 2 * (place - 2) + odd, slot))
            else:
                rows[1].append((k, place - 1 + odd, slot))
        first.append(sorted(rows[0], key=lambda r: r[1]))
        rest.append(sorted(rows[1], key=lambda r: r[1]))
        last.append(sorted(rows[2], key=lambda r: r[1]))
    return table(first), table(rest), table(last)


def bring(sources, places, sems):
    copies = [
        pltpu.make_async_copy(source, place, sems.at[i])
        for i, (source, place) in enumerate(zip(sources, places))
    ]
    for copy in copies:
        copy.start()
    return copies


def encode_kernel(layer, order, *refs):
    *blocks, bias, enc, fire, out, held, weight, mask, shift, acc, sems, wsems, fsem, ssem = refs
    width = blocks[0].shape[1]
    rows = [pl.ds(pl.multiple_of(order[i] * width, width), width) for i in range(8)]
    weights = bring([enc.at[layer, r, :] for r in rows], [weight.at[i] for i in range(8)], wsems)
    values = bring(blocks, [held.at[i] for i in range(8)], sems)
    fired = pltpu.make_async_copy(fire.at[layer], mask, fsem)
    fired.start()
    shifted = pltpu.make_async_copy(bias, shift, ssem)
    shifted.start()
    for i in range(8):
        values[i].wait()
        weights[i].wait()
        term = jnp.dot(held[i], weight[i], preferred_element_type=jnp.float32)
        if i == 0:
            acc[...] = term
        else:
            acc[...] += term
    fired.wait()
    shifted.wait()
    value = acc[...] + shift[layer : layer + 1, :]
    out[...] = (mask[...].astype(jnp.float32) * value).astype(jnp.bfloat16)


def encode(order, blocks, enc, bias, fire, layer):
    tokens, width = blocks[0].shape
    _, depth, feats = enc.shape
    return pl.pallas_call(
        functools.partial(encode_kernel, layer),
        in_specs=[SMEM] + [HBM] * 11,
        out_specs=VMEM,
        out_shape=jax.ShapeDtypeStruct((tokens, feats), jnp.bfloat16),
        scratch_shapes=[
            pltpu.VMEM((8, tokens, width), jnp.bfloat16),
            pltpu.VMEM((8, width, feats), jnp.bfloat16),
            pltpu.VMEM((tokens, feats), jnp.int32),
            pltpu.VMEM(bias.shape, jnp.float32),
            pltpu.VMEM((tokens, feats), jnp.float32),
            pltpu.SemaphoreType.DMA((8,)),
            pltpu.SemaphoreType.DMA((8,)),
            pltpu.SemaphoreType.DMA(()),
            pltpu.SemaphoreType.DMA(()),
        ],
        compiler_params=pltpu.CompilerParams(vmem_limit_bytes=LIMIT),
        cost_estimate=cost(1),
        name="encode",
    )(order, *blocks, bias, enc, fire)


def fetch(entries, dec, ring, sems, i):
    slot = i % SLOTS
    return pltpu.make_async_copy(dec.at[entries[i + 1, 0]], ring.at[slot], sems.at[slot])


def open_stream(entries, dec, ring, sems):
    for i in range(SLOTS):

        @pl.when(i < entries[0, 0])
        def _():
            fetch(entries, dec, ring, sems, i).start()


def run_stream(entries, dec, ring, sems, use):
    count = entries[0, 0]

    def step(i, carry):
        fetch(entries, dec, ring, sems, i).wait()
        use(i + 1, ring.at[i % SLOTS])

        @pl.when(i + SLOTS < count)
        def _():
            fetch(entries, dec, ring, sems, i + SLOTS).start()

        return carry

    lax.fori_loop(0, count, step, 0)


def stream_scratch(dec):
    return [pltpu.VMEM((SLOTS, *dec.shape[1:]), dec.dtype), pltpu.SemaphoreType.DMA((SLOTS,))]


def cost(weight):
    return pl.CostEstimate(flops=weight * 10**9, bytes_accessed=weight * 2**20, transcendentals=0)


def add_pair(acc, slot, acts, dec):
    quarter = dec.shape[1] // 4
    for j in range(4):
        part = slice(j * quarter, (j + 1) * quarter)
        acc[slot, :, part] += jnp.dot(acts, dec[:, part], preferred_element_type=jnp.float32)


def early_kernel(entries, *refs):
    *sources, dec, out, held, acc, hsems, ring, sems = refs
    copies = bring(sources, [held.at[i] for i in range(len(sources))], hsems)
    open_stream(entries, dec, ring, sems)
    acc[...] = jnp.zeros_like(acc)
    for copy in copies:
        copy.wait()

    def use(e, block):
        add_pair(acc, entries[e, 2], held[entries[e, 1]], block)

    run_stream(entries, dec, ring, sems, use)
    out[...] = acc[...].astype(out.dtype)


def reconstruct_early(entries, sources, dec):
    tokens, feats = sources[0].shape
    depth = dec.shape[2]
    return pl.pallas_call(
        early_kernel,
        in_specs=[SMEM] + [HBM] * len(sources) + [HBM],
        out_specs=VMEM,
        scratch_shapes=[
            pltpu.VMEM((len(sources), tokens, feats), jnp.bfloat16),
            pltpu.VMEM((2, tokens, depth), jnp.float32),
            pltpu.SemaphoreType.DMA((len(sources),)),
        ]
        + stream_scratch(dec),
        out_shape=jax.ShapeDtypeStruct((2, tokens, depth), jnp.bfloat16),
        compiler_params=pltpu.CompilerParams(vmem_limit_bytes=LIMIT),
        cost_estimate=cost(10),
        name="reconstruct_early",
    )(entries, *sources, dec)


def late_kernel(entries, cols, *refs):
    *sources, before, dec = refs[:-13]
    outs, (held, acc, hsems, ring, sems) = refs[-13:-5], refs[-5:]
    copies = bring(sources, [held.at[i] for i in range(len(sources))], hsems)
    open_stream(entries, dec, ring, sems)
    acc[...] = jnp.zeros_like(acc)
    tokens, width = outs[0].shape[2:]
    for copy in copies:
        copy.wait()

    def use(e, block):
        add_pair(acc, entries[e, 2], held[entries[e, 1]], block)

    run_stream(entries, dec, ring, sems, use)
    for c in range(CHUNKS):
        rows = slice(c * tokens, (c + 1) * tokens)
        for i in range(8):
            place = pl.ds(pl.multiple_of(cols[i] * width, width), width)
            out = outs[4 * c + i // 2]
            for s in range(2):
                value = acc[s, rows, place] + before[s, rows, place].astype(jnp.float32)
                out[i % 2, s] = value.astype(jnp.bfloat16)


def reconstruct_late(entries, cols, sources, before, dec):
    tokens, feats = sources[0].shape
    depth = dec.shape[2]
    out = jax.ShapeDtypeStruct((2, 2, tokens // CHUNKS, depth // 8), jnp.bfloat16)
    return pl.pallas_call(
        late_kernel,
        in_specs=[SMEM] * 2 + [HBM] * len(sources) + [VMEM, HBM],
        out_specs=[VMEM] * 8,
        scratch_shapes=[
            pltpu.VMEM((len(sources), tokens, feats), jnp.bfloat16),
            pltpu.VMEM((2, tokens, depth), jnp.float32),
            pltpu.SemaphoreType.DMA((len(sources),)),
        ]
        + stream_scratch(dec),
        out_shape=[out] * 8,
        compiler_params=pltpu.CompilerParams(vmem_limit_bytes=LIMIT),
        cost_estimate=cost(10),
        name="reconstruct_late",
    )(entries, cols, *sources, before, dec)


def add_term(entries, e, error, total, block):
    total[entries[e, 1]] += lax.dot_general(
        error[entries[e, 2]], block[...], (((1,), (1,)), ((), ())), preferred_element_type=jnp.float32
    )


def first_kernel(entries, cols, *refs):
    *blocks, dec, two, three, error, total, bsems, ring, sems = refs
    tokens, width = blocks[0].shape[1:]
    places = [pl.ds(pl.multiple_of(cols[j] * width, width), width) for j in range(8)]
    copies = bring(
        blocks,
        [error.at[:, c * tokens : (c + 1) * tokens, p] for c in range(len(blocks) // 8) for p in places],
        bsems,
    )
    open_stream(entries, dec, ring, sems)
    total[...] = jnp.zeros_like(total)
    for copy in copies:
        copy.wait()
    run_stream(
        entries, dec, ring, sems, lambda e, block: add_term(entries, e, error, total, block)
    )
    two[...] = total[:2].astype(two.dtype)
    three[...] = total[2:]


def first_gradients(entries, cols, blocks, dec):
    tokens = blocks[0].shape[1] * (len(blocks) // 8)
    _, feats, depth = dec.shape
    return pl.pallas_call(
        first_kernel,
        in_specs=[SMEM] * 2 + [HBM] * len(blocks) + [HBM],
        out_specs=[VMEM] * 3,
        scratch_shapes=[
            pltpu.VMEM((4, tokens, feats), jnp.float32),
            pltpu.SemaphoreType.DMA((len(blocks),)),
        ]
        + stream_scratch(dec),
        out_shape=[
            jax.ShapeDtypeStruct((2, tokens, feats), jnp.bfloat16),
            jax.ShapeDtypeStruct((2, tokens, feats), jnp.float32),
            jax.ShapeDtypeStruct((2, tokens, depth), jnp.bfloat16),
        ],
        compiler_params=pltpu.CompilerParams(vmem_limit_bytes=LIMIT),
        cost_estimate=cost(10),
        name="first_gradients",
    )(entries, cols, *blocks, dec)


def rest_kernel(entries, whole, begun, dec, one, three, total, ring, sems):
    open_stream(entries, dec, ring, sems)
    total[0:2] = jnp.zeros_like(total[0:2])
    total[2:4] = begun[...]
    run_stream(
        entries, dec, ring, sems, lambda e, block: add_term(entries, e, whole, total, block)
    )
    one[...] = total[:2].astype(one.dtype)
    three[...] = total[2:].astype(three.dtype)


def rest_gradients(entries, whole, begun, dec):
    tokens = whole.shape[1]
    feats = dec.shape[1]
    return pl.pallas_call(
        rest_kernel,
        in_specs=[SMEM, VMEM, VMEM, HBM],
        out_specs=[VMEM] * 2,
        scratch_shapes=[
            pltpu.VMEM((4, tokens, feats), jnp.float32),
        ]
        + stream_scratch(dec),
        out_shape=[jax.ShapeDtypeStruct((2, tokens, feats), jnp.bfloat16)] * 2,
        compiler_params=pltpu.CompilerParams(vmem_limit_bytes=LIMIT),
        cost_estimate=cost(10),
        name="rest_gradients",
    )(entries, whole, begun, dec)


def own_kernel(entries, whole, dec, total, ring, sems):
    open_stream(entries, dec, ring, sems)
    total[...] = jnp.zeros_like(total)
    run_stream(
        entries, dec, ring, sems, lambda e, block: add_term(entries, e, whole, total, block)
    )


def own_gradients(entries, whole, dec):
    tokens = whole.shape[1]
    feats = dec.shape[1]
    return pl.pallas_call(
        own_kernel,
        in_specs=[SMEM, VMEM, HBM],
        out_specs=VMEM,
        scratch_shapes=stream_scratch(dec),
        out_shape=jax.ShapeDtypeStruct((2, tokens, feats), jnp.float32),
        compiler_params=pltpu.CompilerParams(vmem_limit_bytes=LIMIT),
        cost_estimate=cost(10),
        name="own_gradients",
    )(entries, whole, dec)


def after(array, *others):
    return lax.optimization_barrier((array, *others))[0]


def gather(own):
    first = lax.ppermute(own, "feat", FIRST)
    second = lax.ppermute(own, "feat", SECOND)
    both = lax.ppermute(first, "feat", SECOND)
    mine = [own, first, second, both]
    return [*mine, *(lax.ppermute(b, "feat", FLIP) for b in mine)]


def on_device(resid, enc, enc_bias, fire, dec, dec_bias, target):
    f32, bf16 = jnp.float32, jnp.bfloat16
    group = lax.axis_index("layer")
    me = lax.axis_index("feat")
    core = me & 1
    one, two = 2 + 2 * core, 4 - 2 * core
    none = 0 * core
    near = jnp.stack([none, one, two, none + 6, none + 1, two ^ 1, one ^ 1, none + 7])
    columns = (me ^ near).astype(jnp.int32)
    early_table, late_table = (jnp.asarray(t)[group] for t in reconstruct_tables())
    first_table, rest_table, own_table = (jnp.asarray(t)[group] for t in gradient_tables())

    enc, enc_bias, masks = (
        pltpu.with_memory_space_constraint(x, pltpu.HBM) for x in (enc, enc_bias, fire)
    )
    slabs = (resid[0], lax.optimization_barrier(resid)[1])
    ways = []
    for layer in range(2):
        acts = encode(columns, gather(slabs[layer]), enc, enc_bias, masks, layer)
        two_away = lax.ppermute(acts, "layer", TWO)
        nearest = lax.ppermute(acts, "layer", ONE)
        middle = lax.ppermute(acts, "layer", MIDDLE)
        relayed = lax.ppermute(two_away, "layer", RELAY)
        ways.append((acts, nearest, middle, two_away, relayed))
    a, b = ways
    before = reconstruct_early(early_table, [b[0], *a[:4]], dec)
    halves = reconstruct_late(late_table, columns, [*b[1:], a[4]], before, dec)

    tokens = resid.shape[1] // CHUNKS
    errors, blocks = [], []
    for c in range(CHUNKS):
        span = slice(c * tokens, (c + 1) * tokens)
        keep_near, keep_far, send_near, send_far = halves[4 * c : 4 * c + 4]
        far = keep_far.astype(f32) + lax.ppermute(send_far, "feat", FLIP).astype(f32)
        far = lax.ppermute(far.astype(bf16), "feat", SECOND).astype(f32)
        pair = keep_near.astype(f32) + lax.ppermute(send_near, "feat", FLIP).astype(f32)
        close = (pair[1] + far[1]).astype(bf16)
        if errors:
            close = after(close, errors[0])
        close = lax.ppermute(close, "feat", FIRST).astype(f32)
        recon = pair[0] + far[0] + close
        if errors:
            recon = after(recon, errors[0])
        error = recon + dec_bias.astype(f32)[:, None, :] - target[:, span].astype(f32)
        errors.append(error.astype(bf16))
        blocks += gather(errors[c])

    two_away, begun, whole = first_gradients(first_table, columns, blocks, dec)
    mixed = lax.ppermute(two_away, "layer", MIX)
    one_away, three_away = rest_gradients(rest_table, whole, begun, dec)
    ends = lax.ppermute(three_away, "layer", ENDS)
    across = (three_away.astype(f32) + mixed.astype(f32)).astype(bf16)
    middle = lax.ppermute(across, "layer", MIDDLE)
    back = lax.ppermute(one_away, "layer", BACK_ONE)
    own = own_gradients(after(own_table, across), whole, dec)
    inner = (group == 1) | (group == 2)
    here = after(own + jnp.where(inner, 0.0, mixed.astype(f32)))
    total = here + back.astype(f32) + middle.astype(f32) + ends.astype(f32)
    errors[0] = after(errors[0], one_away)
    return jnp.concatenate(errors, axis=1), fire.astype(f32) * total


def solution(mesh):
    placed = (
        P("layer", None, "feat"),
        P("layer", None, "feat"),
        P("layer", "feat"),
        P("layer", None, "feat"),
        P("layer", "feat", None),
        P("layer", "feat"),
        P("layer", None, "feat"),
    )
    blocks = mesh.shape["feat"] == 8 and mesh.shape["layer"] == GROUPS
    return jax.shard_map(
        on_device if blocks else plain,
        mesh=mesh,
        in_specs=placed,
        out_specs=(P("layer", None, "feat"), P("layer", None, "feat")),
        check_vma=False,
    )
```

```python
import functools

import jax
import jax.numpy as jnp
import numpy as np
from jax import lax
from jax.experimental import pallas as pl
from jax.experimental.pallas import tpu as pltpu
from jax.sharding import PartitionSpec as P

LAYERS = 8
GROUPS = 4
VMEM = pl.BlockSpec(memory_space=pltpu.VMEM)
SMEM = pl.BlockSpec(memory_space=pltpu.SMEM)
HBM = pl.BlockSpec(memory_space=pltpu.HBM)
SLOTS = 3
CHUNKS = 2
LIMIT = 32 * 2**20


def plain(resid, enc, enc_bias, fire, dec, dec_bias, target):
    group = lax.axis_index("layer")
    half = LAYERS // 2
    pre = jnp.einsum(
        "ltd,ldf->ltf",
        lax.all_gather(resid, "feat", axis=2, tiled=True),
        enc,
        preferred_element_type=jnp.float32,
    )
    acts = (fire.astype(jnp.float32) * (pre + enc_bias[:, None, :])).astype(jnp.bfloat16)
    every = lax.all_gather(acts, "layer", axis=0, tiled=True)
    order = jnp.arange(LAYERS + 1, dtype=jnp.int32)
    early = order <= group
    source_ids = jnp.where(early, order, order - group - 1)
    chosen = jnp.take(every, source_ids, axis=0)
    lead_mask = early[:half].astype(jnp.bfloat16)[:, None, None]
    lead_acts = chosen[:half]
    low = jnp.einsum(
        "ktf,kfd->td", lead_acts * lead_mask, dec[:half], preferred_element_type=jnp.float32
    )
    high = jnp.einsum(
        "ktf,kfd->td", lead_acts * (1 - lead_mask), dec[:half], preferred_element_type=jnp.float32
    )
    high = high + jnp.einsum(
        "ktf,kfd->td", chosen[half:], dec[half:], preferred_element_type=jnp.float32
    )
    partial_value = jnp.stack([low, high])
    recon = lax.psum(partial_value, "feat")
    whole_target, whole_bias = (
        lax.all_gather(target, "feat", axis=2, tiled=True),
        lax.all_gather(dec_bias, "feat", axis=1, tiled=True),
    )
    wide_error = (
        recon + whole_bias.astype(jnp.float32)[:, None, :] - whole_target.astype(jnp.float32)
    ).astype(jnp.bfloat16)
    columns = target.shape[2]
    error = lax.dynamic_slice_in_dim(wide_error, lax.axis_index("feat") * columns, columns, 2)
    lead_error = jnp.where(early[:half, None, None], wide_error[0][None], wide_error[1][None])
    grads_lead = jnp.einsum(
        "ktd,kfd->ktf", lead_error, dec[:half], preferred_element_type=jnp.float32
    )
    grads_rest = jnp.einsum(
        "td,kfd->ktf", wide_error[1], dec[half:], preferred_element_type=jnp.float32
    )
    pair_grads = jnp.concatenate([grads_lead, grads_rest], axis=0)
    one_hot = (source_ids[:, None] == jnp.arange(LAYERS, dtype=jnp.int32)[None, :]).astype(
        jnp.float32
    )
    grad_terms = jnp.einsum("ks,ktf->stf", one_hot, pair_grads, precision=lax.Precision.HIGHEST)
    summed = lax.psum_scatter(
        grad_terms.astype(jnp.bfloat16), "layer", scatter_dimension=0, tiled=True
    ).astype(jnp.float32)
    act_grad = fire.astype(jnp.float32) * summed
    return (error, act_grad)


ONE = [(0, 1), (1, 0), (2, 3)]
MIDDLE = [(1, 2), (2, 1)]
TWO = [(0, 2), (2, 0), (1, 3), (3, 1)]
RELAY = [(2, 3), (1, 0)]
BUFFER = [[0, 1, 3, 4], [1, 0, 2, 3], [3, 2, 0, 1], [4, 3, 1, 0]]
MIX = [(0, 1), (3, 2), (2, 0), (1, 3)]
ENDS = [(0, 3), (3, 0)]
BACK_ONE = [(0, 1), (1, 0), (3, 2)]
FLIP = [(i, i ^ 1) for i in range(8)]
FIRST = [(i, i ^ (4 if i & 1 else 2)) for i in range(8)]
SECOND = [(i, i ^ (2 if i & 1 else 4)) for i in range(8)]


def pairs_of(group):
    return [(k, k, 0) if k <= group else (k, k - group - 1, 1) for k in range(LAYERS + 1)]


def table(entries):
    out = np.zeros((GROUPS, 1 + max(len(e) for e in entries), 4), np.int32)
    for g, rows in enumerate(entries):
        out[g, 0, 0] = len(rows)
        slots = [slot for _, _, slot in rows]
        for i, row in enumerate(rows):
            out[g, i + 1] = (*row, slots.index(row[2]) == i)
    return out


def reconstruct_tables():
    early, late = [], []
    for g in range(GROUPS):
        rows = ([], [])
        for k, source, slot in pairs_of(g):
            buffer, odd = BUFFER[g][source // 2], source % 2
            if odd and buffer:
                rows[1].append((k, buffer - 1, slot))
            elif buffer == 4:
                rows[1].append((k, 4, slot))
            else:
                rows[0].append((k, 0 if odd else buffer + 1, slot))
        early.append(rows[0])
        late.append(rows[1])
    return table(early), table(late)


def gradient_tables():
    first, rest, last = [], [], []
    for g in range(GROUPS):
        rows = ([], [], [])
        for k, source, slot in pairs_of(g):
            place, odd = source // 2 ^ g, source % 2
            if place == 0:
                rows[2].append((k, odd, slot))
            elif place == 2 or (place == 3 and g < 2):
                rows[0].append((k, 2 * (place - 2) + odd, slot))
            else:
                rows[1].append((k, place - 1 + odd, slot))
        first.append(sorted(rows[0], key=lambda r: r[1]))
        rest.append(sorted(rows[1], key=lambda r: r[1]))
        last.append(sorted(rows[2], key=lambda r: r[1]))
    return table(first), table(rest), table(last)


def bring(sources, places, sems):
    copies = [
        pltpu.make_async_copy(source, place, sems.at[i])
        for i, (source, place) in enumerate(zip(sources, places))
    ]
    for copy in copies:
        copy.start()
    return copies


def encode_kernel(layer, order, *refs):
    *blocks, bias, enc, fire, out, held, weight, mask, shift, acc, sems, wsems, fsem, ssem = refs
    width = blocks[0].shape[1]
    rows = [pl.ds(pl.multiple_of(order[i] * width, width), width) for i in range(8)]
    values, weights = [], []
    for i, block in enumerate(blocks):
        values += bring([block], [held.at[i]], sems.at[pl.ds(i, 1)])
        weights += bring([enc.at[layer, rows[i], :]], [weight.at[i]], wsems.at[pl.ds(i, 1)])
    fired = pltpu.make_async_copy(fire.at[layer], mask, fsem)
    fired.start()
    shifted = pltpu.make_async_copy(bias, shift, ssem)
    shifted.start()
    for i in range(8):
        values[i].wait()
        weights[i].wait()
        term = jnp.dot(held[i], weight[i], preferred_element_type=jnp.float32)
        if i == 0:
            acc[...] = term
        else:
            acc[...] += term
    fired.wait()
    shifted.wait()
    value = acc[...] + shift[layer : layer + 1, :]
    out[...] = (mask[...].astype(jnp.float32) * value).astype(jnp.bfloat16)


def encode(order, blocks, enc, bias, fire, layer):
    tokens, width = blocks[0].shape
    _, depth, feats = enc.shape
    return pl.pallas_call(
        functools.partial(encode_kernel, layer),
        in_specs=[SMEM] + [HBM] * 11,
        out_specs=VMEM,
        out_shape=jax.ShapeDtypeStruct((tokens, feats), jnp.bfloat16),
        scratch_shapes=[
            pltpu.VMEM((8, tokens, width), jnp.bfloat16),
            pltpu.VMEM((8, width, feats), jnp.bfloat16),
            pltpu.VMEM((tokens, feats), jnp.int32),
            pltpu.VMEM(bias.shape, jnp.float32),
            pltpu.VMEM((tokens, feats), jnp.float32),
            pltpu.SemaphoreType.DMA((8,)),
            pltpu.SemaphoreType.DMA((8,)),
            pltpu.SemaphoreType.DMA(()),
            pltpu.SemaphoreType.DMA(()),
        ],
        compiler_params=pltpu.CompilerParams(vmem_limit_bytes=LIMIT),
        cost_estimate=cost(1),
        name="encode",
    )(order, *blocks, bias, enc, fire)


def fetch(entries, dec, ring, sems, i):
    slot = i % SLOTS
    return pltpu.make_async_copy(dec.at[entries[i + 1, 0]], ring.at[slot], sems.at[slot])


def open_stream(entries, dec, ring, sems):
    for i in range(SLOTS):

        @pl.when(i < entries[0, 0])
        def _():
            fetch(entries, dec, ring, sems, i).start()


def run_stream(entries, dec, ring, sems, use):
    count = entries[0, 0]

    def step(i, carry):
        fetch(entries, dec, ring, sems, i).wait()
        use(i + 1, ring.at[i % SLOTS])

        @pl.when(i + SLOTS < count)
        def _():
            fetch(entries, dec, ring, sems, i + SLOTS).start()

        return carry

    lax.fori_loop(0, count, step, 0)


def stream_scratch(dec):
    return [pltpu.VMEM((SLOTS, *dec.shape[1:]), dec.dtype), pltpu.SemaphoreType.DMA((SLOTS,))]


def cost(weight):
    return pl.CostEstimate(flops=weight * 10**9, bytes_accessed=weight * 2**20, transcendentals=0)


def add_pair(acc, slot, acts, dec):
    quarter = dec.shape[1] // 4
    for j in range(4):
        part = slice(j * quarter, (j + 1) * quarter)
        acc[slot, :, part] += jnp.dot(acts, dec[:, part], preferred_element_type=jnp.float32)


def early_kernel(entries, *refs):
    *sources, dec, out, held, acc, hsems, ring, sems = refs
    copies = bring(sources, [held.at[i] for i in range(len(sources))], hsems)
    open_stream(entries, dec, ring, sems)
    acc[...] = jnp.zeros_like(acc)
    for copy in copies:
        copy.wait()

    def use(e, block):
        add_pair(acc, entries[e, 2], held[entries[e, 1]], block)

    run_stream(entries, dec, ring, sems, use)
    out[...] = acc[...].astype(out.dtype)


def reconstruct_early(entries, sources, dec):
    tokens, feats = sources[0].shape
    depth = dec.shape[2]
    return pl.pallas_call(
        early_kernel,
        in_specs=[SMEM] + [HBM] * len(sources) + [HBM],
        out_specs=VMEM,
        scratch_shapes=[
            pltpu.VMEM((len(sources), tokens, feats), jnp.bfloat16),
            pltpu.VMEM((2, tokens, depth), jnp.float32),
            pltpu.SemaphoreType.DMA((len(sources),)),
        ]
        + stream_scratch(dec),
        out_shape=jax.ShapeDtypeStruct((2, tokens, depth), jnp.bfloat16),
        compiler_params=pltpu.CompilerParams(vmem_limit_bytes=LIMIT),
        cost_estimate=cost(10),
        name="reconstruct_early",
    )(entries, *sources, dec)


def late_kernel(entries, cols, *refs):
    *sources, before, dec = refs[:-13]
    outs, (held, acc, hsems, ring, sems) = refs[-13:-5], refs[-5:]
    copies = bring(sources, [held.at[i] for i in range(len(sources))], hsems)
    open_stream(entries, dec, ring, sems)
    acc[...] = jnp.zeros_like(acc)
    tokens, width = outs[0].shape[2:]
    for copy in copies:
        copy.wait()

    def use(e, block):
        add_pair(acc, entries[e, 2], held[entries[e, 1]], block)

    run_stream(entries, dec, ring, sems, use)
    for c in range(CHUNKS):
        rows = slice(c * tokens, (c + 1) * tokens)
        for i in range(8):
            place = pl.ds(pl.multiple_of(cols[i] * width, width), width)
            out = outs[4 * c + i // 2]
            for s in range(2):
                value = acc[s, rows, place] + before[s, rows, place].astype(jnp.float32)
                out[i % 2, s] = value.astype(jnp.bfloat16)


def reconstruct_late(entries, cols, sources, before, dec):
    tokens, feats = sources[0].shape
    depth = dec.shape[2]
    out = jax.ShapeDtypeStruct((2, 2, tokens // CHUNKS, depth // 8), jnp.bfloat16)
    return pl.pallas_call(
        late_kernel,
        in_specs=[SMEM] * 2 + [HBM] * len(sources) + [VMEM, HBM],
        out_specs=[VMEM] * 8,
        scratch_shapes=[
            pltpu.VMEM((len(sources), tokens, feats), jnp.bfloat16),
            pltpu.VMEM((2, tokens, depth), jnp.float32),
            pltpu.SemaphoreType.DMA((len(sources),)),
        ]
        + stream_scratch(dec),
        out_shape=[out] * 8,
        compiler_params=pltpu.CompilerParams(vmem_limit_bytes=LIMIT),
        cost_estimate=cost(10),
        name="reconstruct_late",
    )(entries, cols, *sources, before, dec)


def add_term(entries, e, error, total, block):
    total[entries[e, 1]] += lax.dot_general(
        error[entries[e, 2]], block[...], (((1,), (1,)), ((), ())), preferred_element_type=jnp.float32
    )


def first_kernel(entries, cols, *refs):
    *blocks, dec, two, three, error, total, bsems, ring, sems = refs
    tokens, width = blocks[0].shape[1:]
    places = [pl.ds(pl.multiple_of(cols[j] * width, width), width) for j in range(8)]
    copies = bring(
        blocks,
        [error.at[:, c * tokens : (c + 1) * tokens, p] for c in range(len(blocks) // 8) for p in places],
        bsems,
    )
    open_stream(entries, dec, ring, sems)
    total[...] = jnp.zeros_like(total)
    for copy in copies:
        copy.wait()
    run_stream(
        entries, dec, ring, sems, lambda e, block: add_term(entries, e, error, total, block)
    )
    two[...] = total[:2].astype(two.dtype)
    three[...] = total[2:]


def first_gradients(entries, cols, blocks, dec):
    tokens = blocks[0].shape[1] * (len(blocks) // 8)
    _, feats, depth = dec.shape
    return pl.pallas_call(
        first_kernel,
        in_specs=[SMEM] * 2 + [HBM] * len(blocks) + [HBM],
        out_specs=[VMEM] * 3,
        scratch_shapes=[
            pltpu.VMEM((4, tokens, feats), jnp.float32),
            pltpu.SemaphoreType.DMA((len(blocks),)),
        ]
        + stream_scratch(dec),
        out_shape=[
            jax.ShapeDtypeStruct((2, tokens, feats), jnp.bfloat16),
            jax.ShapeDtypeStruct((2, tokens, feats), jnp.float32),
            jax.ShapeDtypeStruct((2, tokens, depth), jnp.bfloat16),
        ],
        compiler_params=pltpu.CompilerParams(vmem_limit_bytes=LIMIT),
        cost_estimate=cost(10),
        name="first_gradients",
    )(entries, cols, *blocks, dec)


def rest_kernel(entries, whole, begun, dec, one, three, total, ring, sems):
    open_stream(entries, dec, ring, sems)
    total[0:2] = jnp.zeros_like(total[0:2])
    total[2:4] = begun[...]
    run_stream(
        entries, dec, ring, sems, lambda e, block: add_term(entries, e, whole, total, block)
    )
    one[...] = total[:2].astype(one.dtype)
    three[...] = total[2:].astype(three.dtype)


def rest_gradients(entries, whole, begun, dec):
    tokens = whole.shape[1]
    feats = dec.shape[1]
    return pl.pallas_call(
        rest_kernel,
        in_specs=[SMEM, VMEM, VMEM, HBM],
        out_specs=[VMEM] * 2,
        scratch_shapes=[
            pltpu.VMEM((4, tokens, feats), jnp.float32),
        ]
        + stream_scratch(dec),
        out_shape=[jax.ShapeDtypeStruct((2, tokens, feats), jnp.bfloat16)] * 2,
        compiler_params=pltpu.CompilerParams(vmem_limit_bytes=LIMIT),
        cost_estimate=cost(10),
        name="rest_gradients",
    )(entries, whole, begun, dec)


def own_kernel(entries, whole, dec, total, ring, sems):
    open_stream(entries, dec, ring, sems)
    total[...] = jnp.zeros_like(total)
    run_stream(
        entries, dec, ring, sems, lambda e, block: add_term(entries, e, whole, total, block)
    )


def own_gradients(entries, whole, dec):
    tokens = whole.shape[1]
    feats = dec.shape[1]
    return pl.pallas_call(
        own_kernel,
        in_specs=[SMEM, VMEM, HBM],
        out_specs=VMEM,
        scratch_shapes=stream_scratch(dec),
        out_shape=jax.ShapeDtypeStruct((2, tokens, feats), jnp.float32),
        compiler_params=pltpu.CompilerParams(vmem_limit_bytes=LIMIT),
        cost_estimate=cost(10),
        name="own_gradients",
    )(entries, whole, dec)


def after(array, *others):
    return lax.optimization_barrier((array, *others))[0]


def gather(own):
    first = lax.ppermute(own, "feat", FIRST)
    second = lax.ppermute(own, "feat", SECOND)
    both = lax.ppermute(first, "feat", SECOND)
    mine = [own, first, second, both]
    return [*mine, *(lax.ppermute(b, "feat", FLIP) for b in mine)]


def on_device(resid, enc, enc_bias, fire, dec, dec_bias, target):
    f32, bf16 = jnp.float32, jnp.bfloat16
    group = lax.axis_index("layer")
    me = lax.axis_index("feat")
    core = me & 1
    one, two = 2 + 2 * core, 4 - 2 * core
    none = 0 * core
    near = jnp.stack([none, one, two, none + 6, none + 1, two ^ 1, one ^ 1, none + 7])
    columns = (me ^ near).astype(jnp.int32)
    early_table, late_table = (jnp.asarray(t)[group] for t in reconstruct_tables())
    first_table, rest_table, own_table = (jnp.asarray(t)[group] for t in gradient_tables())

    enc, enc_bias, masks = (
        pltpu.with_memory_space_constraint(x, pltpu.HBM) for x in (enc, enc_bias, fire)
    )
    slabs = (resid[0], lax.optimization_barrier(resid)[1])
    ways = []
    for layer in range(2):
        acts = encode(columns, gather(slabs[layer]), enc, enc_bias, masks, layer)
        two_away = lax.ppermute(acts, "layer", TWO)
        nearest = lax.ppermute(acts, "layer", ONE)
        middle = lax.ppermute(acts, "layer", MIDDLE)
        relayed = lax.ppermute(two_away, "layer", RELAY)
        ways.append((acts, nearest, middle, two_away, relayed))
    a, b = ways
    before = reconstruct_early(early_table, [b[0], *a[:4]], dec)
    halves = reconstruct_late(late_table, columns, [*b[1:], a[4]], before, dec)

    tokens = resid.shape[1] // CHUNKS
    errors, blocks = [], []
    for c in range(CHUNKS):
        span = slice(c * tokens, (c + 1) * tokens)
        keep_near, keep_far, send_near, send_far = halves[4 * c : 4 * c + 4]
        far = keep_far.astype(f32) + lax.ppermute(send_far, "feat", FLIP).astype(f32)
        far = lax.ppermute(far.astype(bf16), "feat", SECOND).astype(f32)
        pair = keep_near.astype(f32) + lax.ppermute(send_near, "feat", FLIP).astype(f32)
        close = (pair[1] + far[1]).astype(bf16)
        if errors:
            close = after(close, errors[0])
        close = lax.ppermute(close, "feat", FIRST).astype(f32)
        recon = pair[0] + far[0] + close
        if errors:
            recon = after(recon, errors[0])
        error = recon + dec_bias.astype(f32)[:, None, :] - target[:, span].astype(f32)
        errors.append(error.astype(bf16))
        blocks += gather(errors[c])

    two_away, begun, whole = first_gradients(first_table, columns, blocks, dec)
    mixed = lax.ppermute(two_away, "layer", MIX)
    one_away, three_away = rest_gradients(rest_table, whole, begun, dec)
    ends = lax.ppermute(three_away, "layer", ENDS)
    across = (three_away.astype(f32) + mixed.astype(f32)).astype(bf16)
    middle = lax.ppermute(across, "layer", MIDDLE)
    back = lax.ppermute(one_away, "layer", BACK_ONE)
    own = own_gradients(after(own_table, across), whole, dec)
    inner = (group == 1) | (group == 2)
    here = after(own + jnp.where(inner, 0.0, mixed.astype(f32)))
    total = here + back.astype(f32) + middle.astype(f32) + ends.astype(f32)
    errors[0] = after(errors[0], one_away)
    return jnp.concatenate(errors, axis=1), fire.astype(f32) * total


def solution(mesh):
    placed = (
        P("layer", None, "feat"),
        P("layer", None, "feat"),
        P("layer", "feat"),
        P("layer", None, "feat"),
        P("layer", "feat", None),
        P("layer", "feat"),
        P("layer", None, "feat"),
    )
    blocks = mesh.shape["feat"] == 8 and mesh.shape["layer"] == GROUPS
    return jax.shard_map(
        on_device if blocks else plain,
        mesh=mesh,
        in_specs=placed,
        out_specs=(P("layer", None, "feat"), P("layer", None, "feat")),
        check_vma=False,
    )
```
